32 devices in a mesh: parts: 2 (over x), seq: 16 (over z, y, core), tensor: 1.
Axes of the slice: x: 2, y: 2, z: 4, core: 2. Of those that a mesh axis runs over, the one named last changes fastest.
Arguments:
- stream_in: bfloat16 [8192, 2048], P(('parts', 'seq')), parts along dimension 0, may hold values from -6 to 6
- mr_features: bfloat16 [8192, 3, 2048], P(('parts', 'seq'), None, 'tensor'), parts along dimension 0, may hold values from -6 to 6
- mr_short: float32 [7, 3, 2048], P(None, None, 'tensor'), may hold values from -2 to 2
- medium_taps: float32 [128, 128], replicated, may hold values from -0.5 to 0.5
- mr_out_weight: bfloat16 [2048, 2048], P('tensor', 'seq'), may hold values from -0.125 to 0.125
- li_gain: float32 [2048], replicated, may hold values from 0.1 to 1.9
- li_in_weight: bfloat16 [2048, 3, 2048], P('seq', None, 'tensor'), may hold values from -0.125 to 0.125
- li_short: float32 [7, 3, 2048], P(None, None, 'tensor'), may hold values from -2 to 2
- li_rates: float32 [128, 16], replicated, may hold values from 0 to 1, as said below
- li_residues: float32 [128, 16], replicated, may hold values from -4 to 4
Outputs:
- stream: bfloat16 [8192, 2048], P(('parts', 'seq')), parts along dimension 0
- gated_li: bfloat16 [8192, 2048], P(('parts', 'seq'), 'tensor'), parts along dimension 0
The draws below stay inside these ranges and needn't reach their ends.
There are 2 independent parts, one for each index of `parts`. The reference program is written for one: setup_inputs(seed, part) draws one part's arguments, and reference() takes and returns one part's arrays. A program takes and returns all parts, laid end to end along the dimension named above; an argument that names none is the same for every part. Nothing has to cross between parts.
Inputs may be any that keep to these rules, and one draw needn't show every extreme that they name: `li_rates`: positive decay rates.
All inputs are finite; a program needn't handle non-finite values.
Results may differ from the reference program's by a relative error of at most 0.024.
Values may be sent and summed in bfloat16 or wider, within the bound.
A program may use at most 128 MiB of HBM per device.

```python
import math
import jax
import jax.numpy as jnp
from jax import lax

D = 2048
GROUP = 16
FILTERS = 128
ORDER = 16
SHORT = 7
MEDIUM = 128
SEQLEN = 4096


def draw_li_rates(key, part):
    key = jax.random.fold_in(key, 11)
    lower = math.log(0.5 / SEQLEN)
    upper = math.log(1.0 / 30.0)
    uniform_draw = jax.random.uniform(key, (FILTERS, ORDER), jnp.float32)
    return jnp.exp(lower + (upper - lower) * uniform_draw)


def block_levels(key, extent, shards, least, top_value):
    level = 1.0
    for dim, shards_of in shards:
        heights = jax.random.uniform(jax.random.fold_in(jax.random.fold_in(key, 6), dim), (shards_of,), jnp.float32, least / len(shards), top_value / len(shards))
        level = level * jnp.repeat(jnp.exp(heights), extent[dim] // shards_of).reshape((-1,) + (1,) * (len(extent) - 1 - dim))
    return level


def centred(own_key, extent, deviation, most, shards=(), kind=jnp.bfloat16):
    drawn = deviation * jax.random.normal(own_key, extent, jnp.float32)
    if shards:
        drawn = drawn * block_levels(own_key, extent, shards, -0.22, 0.18)
    return jnp.clip(drawn, -most, most).astype(kind)


def setup_inputs(seed: int = 0, part: int = 0) -> dict:
    keys = jax.random.split(jax.random.key(seed), 11)
    own_keys = jax.random.split(jax.random.fold_in(keys[10], part), 11)
    return {
        "stream_in": centred(own_keys[0], (SEQLEN, D), 1.0, 6.0, ((0, 16),)),
        "mr_features": centred(own_keys[1], (SEQLEN, 3, D), 1.0, 6.0, ((0, 16),)),
        "mr_short": centred(keys[2], (SHORT, 3, D), SHORT ** -0.5, 2.0, (), jnp.float32),
        "medium_taps": centred(keys[3], (MEDIUM, FILTERS), MEDIUM ** -0.5, 0.5, (), jnp.float32),
        "mr_out_weight": centred(keys[4], (D, D), D ** -0.5, 0.125, ((1, 16),)),
        "li_gain": jnp.clip(1.0 + 0.18 * jax.random.normal(keys[5], (D,), jnp.float32), 0.1, 1.9),
        "li_in_weight": centred(keys[6], (D, 3, D), D ** -0.5, 0.125, ((0, 16),)),
        "li_short": centred(keys[7], (SHORT, 3, D), SHORT ** -0.5, 2.0, (), jnp.float32),
        "li_rates": draw_li_rates(jax.random.fold_in(keys[10], 71), part),
        "li_residues": centred(keys[9], (FILTERS, ORDER), 1.0, 4.0, (), jnp.float32),
    }


def root_norm(values, gain_vector):
    widened = values.astype(jnp.float32)
    mean_square = lax.optimization_barrier(jnp.mean(widened * widened, axis=-1, keepdims=True))
    return (widened * lax.rsqrt(mean_square + 1e-06) * gain_vector).astype(jnp.bfloat16)

def short_filter(projected, filter_taps):
    length = projected.shape[0]
    widened = projected.astype(jnp.float32)
    padded = jnp.pad(widened, ((SHORT - 1, 0), (0, 0), (0, 0)))
    running = jnp.zeros(widened.shape, jnp.float32)
    for lagged in range(SHORT):
        running = running + filter_taps[lagged] * padded[SHORT - 1 - lagged:SHORT - 1 - lagged + length]
    return running

def medium_filter(product, filter_taps):
    length = product.shape[0]
    per_channel = jnp.repeat(filter_taps, GROUP, axis=1)
    padded = jnp.pad(product.astype(jnp.float32), ((MEDIUM - 1, 0), (0, 0)))

    def advance(lagged, running):
        window = lax.dynamic_slice_in_dim(padded, MEDIUM - 1 - lagged, length, 0)
        weights = lax.dynamic_index_in_dim(per_channel, lagged, 0, keepdims=False)
        return running + weights * window
    return lax.fori_loop(0, MEDIUM, advance, jnp.zeros(product.shape, jnp.float32))

def long_filter(product, decay_rates, residues):
    length = product.shape[0]
    scaled = residues * jnp.sqrt(2.0 * decay_rates / ORDER)
    offsets = jnp.arange(length, dtype=jnp.float32)
    kernel = jnp.zeros((decay_rates.shape[0], length), jnp.float32)
    for mode_idx in range(ORDER):
        kernel = kernel + scaled[:, mode_idx:mode_idx + 1] * jnp.exp(-decay_rates[:, mode_idx:mode_idx + 1] * offsets)
    padded_len = 2 * length
    kernel_freq = jnp.fft.rfft(kernel, n=padded_len, axis=1)
    signal_freq = jnp.fft.rfft(product.astype(jnp.float32), n=padded_len, axis=0)
    joined = signal_freq * jnp.repeat(kernel_freq.T, GROUP, axis=1)
    return jnp.fft.irfft(joined, n=padded_len, axis=0)[:length]

def reference(stream_in, mr_features, mr_short, medium_taps, mr_out_weight, li_gain, li_in_weight, li_short, li_rates, li_residues):
    filtered = short_filter(mr_features, mr_short)
    product = (filtered[:, 1] * filtered[:, 2]).astype(jnp.bfloat16)
    gated_mr = (filtered[:, 0] * medium_filter(product, medium_taps)).astype(jnp.bfloat16)
    update = jnp.dot(gated_mr, mr_out_weight, preferred_element_type=jnp.float32)
    stream = (stream_in.astype(jnp.float32) + update).astype(jnp.bfloat16)
    normed = root_norm(stream, li_gain)
    channels = li_in_weight.shape[0]
    projected = jnp.dot(normed, li_in_weight.reshape(channels, 3 * channels), preferred_element_type=jnp.float32)
    projected = projected.astype(jnp.bfloat16).reshape(normed.shape[0], 3, channels)
    filtered = short_filter(projected, li_short)
    product = (filtered[:, 1] * filtered[:, 2]).astype(jnp.bfloat16)
    response = long_filter(product, li_rates, li_residues).astype(jnp.bfloat16)
    gated_li = (filtered[:, 0] * response.astype(jnp.float32)).astype(jnp.bfloat16)
    return (stream, gated_li)
```

```python
import functools

import jax
import jax.numpy as jnp
from jax import lax
from jax.experimental import pallas as pl
from jax.experimental.pallas import tpu as pltpu
from jax.sharding import PartitionSpec as P

GROUP = 16
ORDER = 16
SHORT = 7
MEDIUM = 128
BLK = 128
LANES = 128
PER = LANES // GROUP
RIM = 16
bf16 = jnp.bfloat16
f32 = jnp.float32


def cost(flops, nbytes):
    return pl.CostEstimate(flops=flops, bytes_accessed=nbytes, transcendentals=0)


def params():
    return pltpu.CompilerParams(vmem_limit_bytes=40 * 1024 * 1024)


def toeplitz_kernel(base_ref, out_ref):
    row = lax.broadcasted_iota(jnp.int32, (BLK, 2 * BLK), 0)
    col = lax.broadcasted_iota(jnp.int32, (BLK, 2 * BLK), 1)
    causal = col <= row + BLK
    for g in range(PER):
        wide = jnp.broadcast_to(base_ref[g : g + 1, :], (BLK, 2 * BLK))
        rolled = pltpu.roll(wide, 0, 1, stride=1, stride_axis=0)
        out_ref[g * BLK : (g + 1) * BLK, :] = jnp.where(causal, rolled, 0.0).astype(bf16)


def toeplitz(kernel_taps):
    filters = kernel_taps.shape[0]
    base = jnp.roll(kernel_taps[:, ::-1], BLK + 1, axis=1)
    return pl.pallas_call(
        toeplitz_kernel,
        grid=(filters // PER,),
        in_specs=[pl.BlockSpec((PER, 2 * BLK), lambda i: (i, 0))],
        out_specs=pl.BlockSpec((PER * BLK, 2 * BLK), lambda i: (i, 0)),
        out_shape=jax.ShapeDtypeStruct((filters * BLK, 2 * BLK), bf16),
        compiler_params=params(),
        cost_estimate=cost(0, filters * BLK * 2 * BLK * 4),
        name="toeplitz",
    )(base)


def pick(result):
    lane = lax.broadcasted_iota(jnp.int32, (BLK, 2 * LANES), 1) % LANES // GROUP
    total = result[:BLK]
    for g in range(1, PER):
        total = jnp.where(lane == g, result[g * BLK : (g + 1) * BLK], total)
    return total


def two_blocks(table, before, first, second):
    wide = jnp.concatenate(
        [jnp.concatenate([before, first], axis=0), jnp.concatenate([first, second], axis=0)], axis=1
    )
    result = pick(jnp.dot(table, wide, preferred_element_type=f32))
    return result[:, :LANES], result[:, LANES:]


def fir(values, taps, start, length):
    total = taps[0:1] * values[start : start + length]
    for lagged in range(1, SHORT):
        total = total + taps[lagged : lagged + 1] * values[start - lagged : start - lagged + length]
    return total


def medium_kernel(x_ref, taps_ref, table_ref, out_ref):
    rows = x_ref.shape[1]
    own = rows - BLK - RIM
    feats = [x_ref[i].astype(f32) for i in range(3)]
    q = fir(feats[0], taps_ref[0], BLK + RIM, own)
    k = fir(feats[1], taps_ref[1], RIM, own + BLK)
    v = fir(feats[2], taps_ref[2], RIM, own + BLK)
    product = (k * v).astype(bf16)
    table = table_ref[...]
    for n in range(0, own // BLK, 2):
        part = [product[(n + j) * BLK : (n + j + 1) * BLK] for j in range(3)]
        y0, y1 = two_blocks(table, *part)
        out_ref[n * BLK : (n + 1) * BLK] = (q[n * BLK : (n + 1) * BLK] * y0).astype(bf16)
        out_ref[(n + 1) * BLK : (n + 2) * BLK] = (q[(n + 1) * BLK : (n + 2) * BLK] * y1).astype(bf16)


def medium(extended, taps, table):
    _, rows, channels = extended.shape
    own = rows - BLK - RIM
    return pl.pallas_call(
        medium_kernel,
        grid=(channels // LANES,),
        in_specs=[
            pl.BlockSpec((3, rows, LANES), lambda i: (0, 0, i)),
            pl.BlockSpec((3, SHORT, LANES), lambda i: (0, 0, i)),
            pl.BlockSpec((PER * BLK, 2 * BLK), lambda i: (i, 0)),
        ],
        out_specs=pl.BlockSpec((own, LANES), lambda i: (0, i)),
        out_shape=jax.ShapeDtypeStruct((own, channels), bf16),
        compiler_params=params(),
        cost_estimate=cost(channels // LANES * 2 * 1024 * 256 * 256, 16 * 2**20),
        name="medium",
    )(extended, taps, table)


def product_kernel(segs, k_ref, v_ref, taps_ref, high_ref, low_ref, product_ref, state_ref):
    rows = k_ref.shape[1] - RIM
    seg = rows // segs
    k = fir(k_ref[0].astype(f32), taps_ref[1], RIM, rows)
    v = fir(v_ref[0].astype(f32), taps_ref[2], RIM, rows)
    product = (k * v).astype(bf16)
    product_ref[0] = product
    lane = lax.broadcasted_iota(jnp.int32, (ORDER, LANES), 1) // GROUP
    for s in range(segs):
        part = product[s * seg : (s + 1) * seg]
        sums = jnp.dot(high_ref[...], part, preferred_element_type=f32) + jnp.dot(
            low_ref[...], part, preferred_element_type=f32
        )
        total = sums[:ORDER]
        for g in range(1, PER):
            total = jnp.where(lane == g, sums[g * ORDER : (g + 1) * ORDER], total)
        state_ref[0, s] = total


def local_kernel(segs, q_ref, taps_ref, product_ref, table_ref, q_out, y_out):
    rows = q_ref.shape[1] - RIM
    seg = rows // segs
    q_out[0] = fir(q_ref[0].astype(f32), taps_ref[0], RIM, rows)
    zeros = jnp.zeros((BLK, LANES), bf16)
    table = table_ref[...]
    for s in range(segs):
        first = product_ref[0, s * seg : s * seg + BLK]
        second = product_ref[0, s * seg + BLK : (s + 1) * seg]
        y0, y1 = two_blocks(table, zeros, first, second)
        y_out[0, s * seg : s * seg + BLK] = y0
        y_out[0, s * seg + BLK : (s + 1) * seg] = y1


def finish_kernel(segs, q_ref, y_ref, state_ref, high_ref, low_ref, out_ref):
    seg = q_ref.shape[1] // segs
    row = lax.broadcasted_iota(jnp.int32, (LANES, LANES), 0) // ORDER
    lane = lax.broadcasted_iota(jnp.int32, (LANES, LANES), 1) // GROUP
    for s in range(segs):
        state = jnp.concatenate([state_ref[0, s]] * PER, axis=0)
        state = jnp.where(row == lane, state, 0.0)
        state_high = state.astype(bf16)
        state_low = (state - state_high.astype(f32)).astype(bf16)
        at = slice(s * seg, (s + 1) * seg)
        y = y_ref[0, at]
        y = y + jnp.dot(high_ref[...], state_high, preferred_element_type=f32)
        y = y + jnp.dot(high_ref[...], state_low, preferred_element_type=f32)
        y = y + jnp.dot(low_ref[...], state_high, preferred_element_type=f32)
        out_ref[0, at] = (q_ref[0, at] * y.astype(bf16).astype(f32)).astype(bf16)


def long_product(projected, taps, high, low, segs):
    groups, rows, channels = projected.shape
    channels //= 3
    blocks = channels // LANES
    own = rows - RIM
    seg = own // segs
    return pl.pallas_call(
        functools.partial(product_kernel, segs),
        grid=(blocks, groups),
        in_specs=[
            pl.BlockSpec((1, rows, LANES), lambda i, x: (x, 0, blocks + i)),
            pl.BlockSpec((1, rows, LANES), lambda i, x: (x, 0, 2 * blocks + i)),
            pl.BlockSpec((3, SHORT, LANES), lambda i, x: (0, 0, i)),
            pl.BlockSpec((PER * ORDER, seg), lambda i, x: (i, 0)),
            pl.BlockSpec((PER * ORDER, seg), lambda i, x: (i, 0)),
        ],
        out_specs=[
            pl.BlockSpec((1, own, LANES), lambda i, x: (x, 0, i)),
            pl.BlockSpec((1, segs, ORDER, LANES), lambda i, x: (x, 0, 0, i)),
        ],
        out_shape=[
            jax.ShapeDtypeStruct((groups, own, channels), bf16),
            jax.ShapeDtypeStruct((groups, segs, ORDER, channels), f32),
        ],
        compiler_params=params(),
        cost_estimate=cost(2**28, 8 * 2**20),
        name="product",
    )(projected, projected, taps, high, low)


def long_local(projected, taps, product, table, segs):
    groups, rows, channels = projected.shape
    channels //= 3
    own = rows - RIM
    whole = pl.BlockSpec((1, own, LANES), lambda i, x: (x, 0, i))
    return pl.pallas_call(
        functools.partial(local_kernel, segs),
        grid=(channels // LANES, groups),
        in_specs=[
            pl.BlockSpec((1, rows, LANES), lambda i, x: (x, 0, i)),
            pl.BlockSpec((3, SHORT, LANES), lambda i, x: (0, 0, i)),
            whole,
            pl.BlockSpec((PER * BLK, 2 * BLK), lambda i, x: (i, 0)),
        ],
        out_specs=[whole, whole],
        out_shape=[jax.ShapeDtypeStruct((groups, own, channels), f32)] * 2,
        compiler_params=params(),
        cost_estimate=cost(2**31, 16 * 2**20),
        name="local",
    )(projected, taps, product, table)


def long_finish(q, y, state, high, low, segs):
    groups, own, channels = q.shape
    seg = own // segs
    whole = pl.BlockSpec((1, own, LANES), lambda i, x: (x, 0, i))
    decay = pl.BlockSpec((seg, PER * ORDER), lambda i, x: (0, i))
    return pl.pallas_call(
        functools.partial(finish_kernel, segs),
        grid=(channels // LANES, groups),
        in_specs=[
            whole,
            whole,
            pl.BlockSpec((1, segs, ORDER, LANES), lambda i, x: (x, 0, 0, i)),
            decay,
            decay,
        ],
        out_specs=whole,
        out_shape=jax.ShapeDtypeStruct((groups, own, channels), bf16),
        compiler_params=params(),
        cost_estimate=cost(2**28, 8 * 2**20),
        name="finish",
    )(q, y, state, high, low)


def split_high_low(value):
    high = lax.reduce_precision(value, 8, 7)
    return high.astype(bf16), (value - high).astype(bf16)


def shift_seq(value, steps):
    count = lax.axis_size("seq")
    return lax.ppermute(value, "seq", [(s, s + steps) for s in range(count - steps)])


def pair_stack(mine, other, index):
    first = index == 0
    return jnp.stack([jnp.where(first, mine, other), jnp.where(first, other, mine)])


def ring_order(chips):
    if chips % 2:
        return list(range(chips))
    return list(range(0, chips, 2)) + list(range(chips - 1, 0, -2))


def ring_gather(up, down, cores, after=None):
    count = lax.axis_size("seq")
    chips = count // cores
    order = ring_order(chips)
    spot = [order.index(chip) for chip in range(chips)]
    chip = lax.axis_index("seq") // cores
    place = jnp.asarray(spot, jnp.int32)[chip]
    lookup = jnp.asarray(order, jnp.int32)

    def perm(step):
        return [
            (order[a] * cores + c, order[(a + step) % chips] * cores + c)
            for a in range(chips)
            for c in range(cores)
        ]

    def put(store, piece, owner):
        return lax.dynamic_update_slice_in_dim(store, piece[None], owner, 0)

    both = [jnp.zeros((chips,) + up.shape, up.dtype), jnp.zeros((chips,) + down.shape, down.dtype)]
    both = [put(both[0], up, chip), put(both[1], down, chip)]
    for step in range(1, chips):
        up = lax.ppermute(up, "seq", perm(1))
        down = lax.ppermute(down, "seq", perm(-1))
        both[0] = put(both[0], up, lookup[(place - step) % chips])
        both[1] = put(both[1], down, lookup[(place + step) % chips])
    return both, up, down


def body(
    stream_in,
    mr_features,
    mr_short,
    medium_taps,
    mr_out_weight,
    li_gain,
    li_in_weight,
    li_short,
    li_rates,
    li_residues,
):
    rows = stream_in.shape[0]
    width = stream_in.shape[1]
    channels = mr_features.shape[2]
    tensors = lax.axis_size("tensor")
    cores = 2 if tensors == 1 and lax.axis_size("seq") % 4 == 0 else 1
    wide = 2 if cores == 2 and lax.axis_size("parts") == 2 else 1
    share = cores * wide
    count = lax.axis_size("seq")
    chips = count // cores
    seq_rank = lax.axis_index("seq")
    core = seq_rank % cores
    side = lax.axis_index("parts") if wide == 2 else 0
    tensor_rank = lax.axis_index("tensor")
    swap_pairs = [(s, s ^ 1) for s in range(count)]

    def swap_core(value):
        return lax.ppermute(value, "seq", swap_pairs)

    def swap_side(value):
        return lax.ppermute(value, "parts", [(0, 1), (1, 0)])

    part = channels // share
    quarter = side * cores + core
    filters = part // GROUP
    first_filter = tensor_rank * (channels // GROUP) + quarter * filters

    rim = shift_seq(jnp.transpose(mr_features[rows - BLK - RIM :], (1, 0, 2)), 1)
    extended = jnp.concatenate([rim, jnp.transpose(mr_features, (1, 0, 2))], axis=1)

    if cores == 2:
        half = width // 2
        out_stacks, last_up, last_down = ring_gather(
            mr_out_weight[: channels // 2], mr_out_weight[channels // 2 :], cores
        )
        weight = li_in_weight.reshape(-1, 3, share, part)
        mine = lax.dynamic_index_in_dim(weight, side * cores + core, 2, keepdims=False)
        theirs = lax.dynamic_index_in_dim(weight, side * cores + 1 - core, 2, keepdims=False)
        mine = mine.reshape(-1, 3 * part)
        other = swap_core(theirs.reshape(-1, 3 * part))
        halves = pair_stack(mine, other, core)
        up, down, last_up, last_down = lax.optimization_barrier(
            (halves[0], halves[1], last_up, last_down)
        )
        in_stacks, _, _ = ring_gather(up, down, cores)
        in_weight = jnp.stack(in_stacks, axis=1).reshape(width, 3 * part)
    else:
        out_weight = lax.all_gather(mr_out_weight, "seq", axis=1, tiled=True)
        in_weight = lax.all_gather(li_in_weight, "seq", axis=0, tiled=True).reshape(width, -1)

    local_taps = lax.dynamic_slice_in_dim(
        medium_taps, tensor_rank * (channels // GROUP), channels // GROUP, 1
    )
    medium_table = toeplitz(jnp.pad(local_taps.T, ((0, 0), (0, 2 * BLK - MEDIUM))))
    rates = lax.dynamic_slice_in_dim(li_rates, first_filter, filters, 0)
    residues = lax.dynamic_slice_in_dim(li_residues, first_filter, filters, 0)
    scaled = residues * jnp.sqrt(2.0 * rates / ORDER)
    steps = jnp.arange(rows, dtype=f32)
    spread = scaled.reshape(1, -1) * jnp.exp(-rates.reshape(1, -1) * steps[:, None])
    long_table = toeplitz(jnp.sum(spread.reshape(rows, filters, ORDER), axis=-1).T)
    spread_high, spread_low = split_high_low(spread)
    tail = jnp.exp(-rates.reshape(-1, 1) * (rows - steps)[None, :])
    tail_high, tail_low = split_high_low(tail)
    by_channel = jnp.repeat(rates.T, GROUP, axis=1)
    seg_decay = jnp.exp(-by_channel * rows)
    gap_decays = [jnp.exp(-by_channel * (rows * cores * gap)) for gap in range(chips - 1)]
    short_part = lax.dynamic_slice_in_dim(li_short, quarter * part, part, 2)
    short_part = jnp.transpose(short_part, (1, 0, 2))

    gated = medium(extended, jnp.transpose(mr_short, (1, 0, 2)), medium_table)

    if cores == 2:
        both = pair_stack(gated, swap_core(gated), core).reshape(cores * rows, channels)
        update = sum(
            jnp.einsum(
                "rk,jkn->jrn",
                both[:, i * channels // 2 : (i + 1) * channels // 2],
                out_stacks[i],
                preferred_element_type=f32,
            )
            for i in range(2)
        )
        update = update.reshape(chips, cores, rows, -1)
        mine = lax.dynamic_index_in_dim(update, core, 1, keepdims=False)
        theirs = lax.dynamic_index_in_dim(update, 1 - core, 1, keepdims=False)
        update = pair_stack(mine, swap_core(theirs), core)
        summed = jnp.transpose(update, (2, 1, 0, 3)).reshape(rows, width)
    else:
        summed = lax.psum(jnp.dot(gated, out_weight, preferred_element_type=f32), "tensor")
    stream = (stream_in.astype(f32) + summed).astype(bf16)
    widened = stream.astype(f32)
    mean_square = jnp.mean(widened * widened, axis=-1, keepdims=True)
    normed = (widened * lax.rsqrt(mean_square + 1e-06) * li_gain).astype(bf16)

    rows_all = normed[None]
    if wide == 2:
        rows_all = pair_stack(normed, swap_side(normed), side)
    if cores == 2:
        rows_all = pair_stack(rows_all, swap_core(rows_all), core)
        rows_all = jnp.transpose(rows_all, (1, 0, 2, 3)).reshape(wide, cores * rows, width)
    ahead = shift_seq(rows_all[:, cores * rows - RIM :], cores)
    rows_all = jnp.concatenate([ahead, rows_all], axis=1)
    projected = jnp.dot(
        rows_all.reshape(-1, width), in_weight, preferred_element_type=f32
    ).astype(bf16)
    projected = projected.reshape(wide, RIM + cores * rows, 3 * part)

    product, added = long_product(projected, short_part, tail_high, tail_low, cores)
    state = added[:, 0]
    for seg in range(1, cores):
        state = state * seg_decay + added[:, seg]
    start = 0.0
    for gap in range(1, chips):
        start = start + gap_decays[gap - 1] * shift_seq(state, gap * cores)
    starts = [start]
    for seg in range(1, cores):
        starts.append(starts[-1] * seg_decay + added[:, seg - 1])
    q, y = long_local(projected, short_part, product, long_table, cores)
    gated_li = long_finish(q, y, jnp.stack(starts, axis=1), spread_high, spread_low, cores)

    result = gated_li
    if wide == 2:
        mine = lax.dynamic_index_in_dim(result, side, 0, keepdims=False)
        theirs = lax.dynamic_index_in_dim(result, 1 - side, 0, keepdims=False)
        result = pair_stack(mine, swap_side(theirs), side)
    if cores == 2:
        result = result.reshape(wide, cores, rows, part)
        mine = lax.dynamic_index_in_dim(result, core, 1, keepdims=False)
        theirs = lax.dynamic_index_in_dim(result, 1 - core, 1, keepdims=False)
        result = pair_stack(mine, swap_core(theirs), core)
        result = jnp.transpose(result, (2, 1, 0, 3)).reshape(rows, channels)
    else:
        result = result.reshape(rows, channels)
    return (stream, result)


def solution(mesh):
    placed = (
        P(("parts", "seq"), None),
        P(("parts", "seq"), None, "tensor"),
        P(None, None, "tensor"),
        P(),
        P("tensor", "seq"),
        P(),
        P("seq", None, "tensor"),
        P(None, None, "tensor"),
        P(),
        P(),
    )
    return jax.shard_map(
        body,
        mesh=mesh,
        in_specs=placed,
        out_specs=(P(("parts", "seq"), None), P(("parts", "seq"), "tensor")),
        check_vma=False,
    )
```

```python
import functools

import jax
import jax.numpy as jnp
from jax import lax
from jax.experimental import pallas as pl
from jax.experimental.pallas import tpu as pltpu
from jax.sharding import PartitionSpec as P

GROUP = 16
ORDER = 16
SHORT = 7
MEDIUM = 128
BLK = 128
LANES = 128
PER = LANES // GROUP
RIM = 16
bf16 = jnp.bfloat16
f32 = jnp.float32


def cost(flops, nbytes):
    return pl.CostEstimate(flops=flops, bytes_accessed=nbytes, transcendentals=0)


def params():
    return pltpu.CompilerParams(vmem_limit_bytes=40 * 1024 * 1024)


def toeplitz_kernel(base_ref, out_ref):
    row = lax.broadcasted_iota(jnp.int32, (BLK, 2 * BLK), 0)
    col = lax.broadcasted_iota(jnp.int32, (BLK, 2 * BLK), 1)
    causal = col <= row + BLK
    for g in range(PER):
        wide = jnp.broadcast_to(base_ref[g : g + 1, :], (BLK, 2 * BLK))
        rolled = pltpu.roll(wide, 0, 1, stride=1, stride_axis=0)
        out_ref[g * BLK : (g + 1) * BLK, :] = jnp.where(causal, rolled, 0.0).astype(bf16)


def toeplitz(kernel_taps):
    filters = kernel_taps.shape[0]
    base = jnp.roll(kernel_taps[:, ::-1], BLK + 1, axis=1)
    return pl.pallas_call(
        toeplitz_kernel,
        grid=(filters // PER,),
        in_specs=[pl.BlockSpec((PER, 2 * BLK), lambda i: (i, 0))],
        out_specs=pl.BlockSpec((PER * BLK, 2 * BLK), lambda i: (i, 0)),
        out_shape=jax.ShapeDtypeStruct((filters * BLK, 2 * BLK), bf16),
        compiler_params=params(),
        cost_estimate=cost(0, filters * BLK * 2 * BLK * 4),
        name="toeplitz",
    )(base)


def pick(result):
    lane = lax.broadcasted_iota(jnp.int32, (BLK, 2 * LANES), 1) % LANES // GROUP
    total = result[:BLK]
    for g in range(1, PER):
        total = jnp.where(lane == g, result[g * BLK : (g + 1) * BLK], total)
    return total


def two_blocks(table, before, first, second):
    wide = jnp.concatenate(
        [jnp.concatenate([before, first], axis=0), jnp.concatenate([first, second], axis=0)], axis=1
    )
    result = pick(jnp.dot(table, wide, preferred_element_type=f32))
    return result[:, :LANES], result[:, LANES:]


def fir(values, taps, start, length):
    total = taps[0:1] * values[start : start + length]
    for lagged in range(1, SHORT):
        total = total + taps[lagged : lagged + 1] * values[start - lagged : start - lagged + length]
    return total


def medium_kernel(x_ref, rim_ref, taps_ref, table_ref, out_ref):
    own = x_ref.shape[1]
    ahead = BLK + RIM

    def joined(at, length, i):
        return jnp.concatenate([rim_ref[at : at + length], x_ref[i]], axis=0).astype(f32)

    q = fir(joined(2 * ahead, RIM, 0), taps_ref[0], RIM, own)
    k = fir(joined(0, ahead, 1), taps_ref[1], RIM, own + BLK)
    v = fir(joined(ahead, ahead, 2), taps_ref[2], RIM, own + BLK)
    product = (k * v).astype(bf16)
    table = table_ref[...]
    for n in range(0, own // BLK, 2):
        part = [product[(n + j) * BLK : (n + j + 1) * BLK] for j in range(3)]
        y0, y1 = two_blocks(table, *part)
        out_ref[n * BLK : (n + 1) * BLK] = (q[n * BLK : (n + 1) * BLK] * y0).astype(bf16)
        out_ref[(n + 1) * BLK : (n + 2) * BLK] = (q[(n + 1) * BLK : (n + 2) * BLK] * y1).astype(bf16)


def medium(features, rim, taps, table):
    _, own, channels = features.shape
    return pl.pallas_call(
        medium_kernel,
        grid=(channels // LANES,),
        in_specs=[
            pl.BlockSpec((3, own, LANES), lambda i: (0, 0, i)),
            pl.BlockSpec((rim.shape[0], LANES), lambda i: (0, i)),
            pl.BlockSpec((3, SHORT, LANES), lambda i: (0, 0, i)),
            pl.BlockSpec((PER * BLK, 2 * BLK), lambda i: (i, 0)),
        ],
        out_specs=pl.BlockSpec((own, LANES), lambda i: (0, i)),
        out_shape=jax.ShapeDtypeStruct((own, channels), bf16),
        compiler_params=params(),
        cost_estimate=cost(channels // LANES * 2 * 1024 * 256 * 256, 16 * 2**20),
        name="medium",
    )(features, rim, taps, table)


def out_kernel(a_ref, b_ref, *refs):
    pieces, (mine, theirs) = refs[:-2], refs[-2:]
    for n in range(0, len(pieces), 2):
        weight = jnp.concatenate([pieces[n][...], pieces[n + 1][...]], axis=1)
        for source, target in ((a_ref, mine), (b_ref, theirs)):
            result = jnp.dot(source[...], weight, preferred_element_type=f32)
            half = result.shape[1] // 2
            target[n] = result[:, :half]
            target[n + 1] = result[:, half:]


def out_projection(gated, other, pieces):
    rows = gated.shape[0]
    shape = jax.ShapeDtypeStruct((len(pieces), rows, pieces[0].shape[1]), f32)
    return pl.pallas_call(
        out_kernel,
        out_shape=[shape, shape],
        compiler_params=params(),
        cost_estimate=cost(2**31, 9 * 2**20),
        name="out_projection",
    )(gated, other, *pieces)


def stream_kernel(where_ref, mine_ref, recv_ref, in_ref, gain_ref, stream_ref, normed_ref):
    chips, rows, piece = mine_ref.shape
    chip, core = where_ref[0], where_ref[1]
    total = jnp.zeros((rows, 1), f32)
    kept = []
    for j in range(chips):
        columns = pl.ds(pl.multiple_of((chip + j) % chips * 2 * piece, 2 * piece), 2 * piece)
        mine, recv = mine_ref[j], recv_ref[j]
        first = jnp.where(core == 0, mine, recv)
        second = jnp.where(core == 0, recv, mine)
        update = jnp.concatenate([first, second], axis=1)
        value = (in_ref[:, columns].astype(f32) + update).astype(bf16)
        stream_ref[:, columns] = value
        value = value.astype(f32)
        total = total + jnp.sum(value * value, axis=1, keepdims=True)
        kept.append((columns, value))
    scale = lax.rsqrt(total / (chips * 2 * piece) + 1e-06)
    for j in range(chips):
        columns, value = kept[j]
        normed_ref[j] = (value * scale * gain_ref[:, columns]).astype(bf16)


def stream_norm(where, mine, recv, stream_in, gain):
    chips, rows, piece = mine.shape
    width = stream_in.shape[1]
    step = 64
    pieces = pl.BlockSpec((chips, step, piece), lambda i: (0, i, 0))
    whole = pl.BlockSpec((step, width), lambda i: (i, 0))
    return pl.pallas_call(
        stream_kernel,
        grid=(rows // step,),
        in_specs=[
            pl.BlockSpec(memory_space=pltpu.SMEM),
            pieces,
            pieces,
            whole,
            pl.BlockSpec((1, width), lambda i: (0, 0)),
        ],
        out_specs=[whole, pl.BlockSpec((chips, step, 2 * piece), lambda i: (0, i, 0))],
        out_shape=[
            jax.ShapeDtypeStruct((rows, width), bf16),
            jax.ShapeDtypeStruct((chips, rows, 2 * piece), bf16),
        ],
        compiler_params=params(),
        cost_estimate=cost(2**22, 6 * 2**20),
        name="stream_norm",
    )(where, mine, recv, stream_in, gain)


def in_kernel(wide, chips, where_ref, ahead_ref, *refs):
    sources, pieces, out_ref = refs[: 2 * wide], refs[2 * wide : -1], refs[-1]
    side, core, chip = where_ref[2], where_ref[1], where_ref[0]
    rows = sources[0].shape[1]

    def times(value):
        total = jnp.dot(value(0), pieces[0][...], preferred_element_type=f32)
        for j in range(1, chips):
            total = total + jnp.dot(value(j), pieces[j][...], preferred_element_type=f32)
        return total

    for off_side in range(wide):
        at = (side + off_side) % wide
        front = times(lambda j: ahead_ref[off_side, j])
        out_ref[at, :RIM] = jnp.where(chip > 0, front, 0.0).astype(bf16)
        for off_core in range(2):
            start = pl.multiple_of(RIM + (core + off_core) % 2 * rows, RIM)
            result = times(lambda j: sources[off_side * 2 + off_core][j])
            out_ref[at, pl.ds(start, rows)] = result.astype(bf16)


def in_projection(where, ahead, sources, pieces):
    wide = len(sources) // 2
    chips, rows, depth = sources[0].shape
    columns = pieces[0].shape[1]
    step = 256
    fixed = pl.BlockSpec((chips, rows, depth), lambda n: (0, 0, 0))
    total = RIM + 2 * rows
    return pl.pallas_call(
        functools.partial(in_kernel, wide, chips),
        grid=(columns // step,),
        in_specs=[
            pl.BlockSpec(memory_space=pltpu.SMEM),
            pl.BlockSpec(ahead.shape, lambda n: (0, 0, 0, 0)),
        ]
        + [fixed] * len(sources)
        + [pl.BlockSpec((depth, step), lambda n: (0, n))] * chips,
        out_specs=pl.BlockSpec((wide, total, step), lambda n: (0, 0, n)),
        out_shape=jax.ShapeDtypeStruct((wide, total, columns), bf16),
        compiler_params=params(),
        cost_estimate=cost(2 * wide * total * chips * depth * columns, 14 * 2**20),
        name="in_projection",
    )(where, ahead, *sources, *pieces)


def product_kernel(segs, k_ref, v_ref, taps_ref, high_ref, low_ref, product_ref, state_ref):
    rows = k_ref.shape[1] - RIM
    seg = rows // segs
    k = fir(k_ref[0].astype(f32), taps_ref[1], RIM, rows)
    v = fir(v_ref[0].astype(f32), taps_ref[2], RIM, rows)
    product = (k * v).astype(bf16)
    product_ref[0] = product
    lane = lax.broadcasted_iota(jnp.int32, (ORDER, LANES), 1) // GROUP
    for s in range(segs):
        part = product[s * seg : (s + 1) * seg]
        sums = jnp.dot(high_ref[...], part, preferred_element_type=f32) + jnp.dot(
            low_ref[...], part, preferred_element_type=f32
        )
        total = sums[:ORDER]
        for g in range(1, PER):
            total = jnp.where(lane == g, sums[g * ORDER : (g + 1) * ORDER], total)
        state_ref[0, s] = total


def local_kernel(segs, q_ref, taps_ref, product_ref, table_ref, q_out, y_out):
    rows = q_ref.shape[1] - RIM
    seg = rows // segs
    q_out[0] = fir(q_ref[0].astype(f32), taps_ref[0], RIM, rows)
    zeros = jnp.zeros((BLK, LANES), bf16)
    table = table_ref[...]
    for s in range(segs):
        first = product_ref[0, s * seg : s * seg + BLK]
        second = product_ref[0, s * seg + BLK : (s + 1) * seg]
        y0, y1 = two_blocks(table, zeros, first, second)
        y_out[0, s * seg : s * seg + BLK] = y0
        y_out[0, s * seg + BLK : (s + 1) * seg] = y1


def finish_kernel(segs, q_ref, y_ref, state_ref, high_ref, low_ref, out_ref):
    seg = q_ref.shape[1] // segs
    row = lax.broadcasted_iota(jnp.int32, (LANES, LANES), 0) // ORDER
    lane = lax.broadcasted_iota(jnp.int32, (LANES, LANES), 1) // GROUP
    for s in range(segs):
        state = jnp.concatenate([state_ref[0, s]] * PER, axis=0)
        state = jnp.where(row == lane, state, 0.0)
        state_high = state.astype(bf16)
        state_low = (state - state_high.astype(f32)).astype(bf16)
        at = slice(s * seg, (s + 1) * seg)
        y = y_ref[0, at]
        y = y + jnp.dot(high_ref[...], state_high, preferred_element_type=f32)
        y = y + jnp.dot(high_ref[...], state_low, preferred_element_type=f32)
        y = y + jnp.dot(low_ref[...], state_high, preferred_element_type=f32)
        out_ref[0, at] = (q_ref[0, at] * y.astype(bf16).astype(f32)).astype(bf16)


def long_product(projected, taps, high, low, segs):
    groups, rows, channels = projected.shape
    channels //= 3
    blocks = channels // LANES
    own = rows - RIM
    seg = own // segs
    return pl.pallas_call(
        functools.partial(product_kernel, segs),
        grid=(blocks, groups),
        in_specs=[
            pl.BlockSpec((1, rows, LANES), lambda i, x: (x, 0, blocks + i)),
            pl.BlockSpec((1, rows, LANES), lambda i, x: (x, 0, 2 * blocks + i)),
            pl.BlockSpec((3, SHORT, LANES), lambda i, x: (0, 0, i)),
            pl.BlockSpec((PER * ORDER, seg), lambda i, x: (i, 0)),
            pl.BlockSpec((PER * ORDER, seg), lambda i, x: (i, 0)),
        ],
        out_specs=[
            pl.BlockSpec((1, own, LANES), lambda i, x: (x, 0, i)),
            pl.BlockSpec((1, segs, ORDER, LANES), lambda i, x: (x, 0, 0, i)),
        ],
        out_shape=[
            jax.ShapeDtypeStruct((groups, own, channels), bf16),
            jax.ShapeDtypeStruct((groups, segs, ORDER, channels), f32),
        ],
        compiler_params=params(),
        cost_estimate=cost(2**28, 8 * 2**20),
        name="product",
    )(projected, projected, taps, high, low)


def long_local(projected, taps, product, table, segs):
    groups, rows, channels = projected.shape
    channels //= 3
    own = rows - RIM
    whole = pl.BlockSpec((1, own, LANES), lambda i, x: (x, 0, i))
    return pl.pallas_call(
        functools.partial(local_kernel, segs),
        grid=(channels // LANES, groups),
        in_specs=[
            pl.BlockSpec((1, rows, LANES), lambda i, x: (x, 0, i)),
            pl.BlockSpec((3, SHORT, LANES), lambda i, x: (0, 0, i)),
            whole,
            pl.BlockSpec((PER * BLK, 2 * BLK), lambda i, x: (i, 0)),
        ],
        out_specs=[whole, whole],
        out_shape=[jax.ShapeDtypeStruct((groups, own, channels), f32)] * 2,
        compiler_params=params(),
        cost_estimate=cost(2**31, 16 * 2**20),
        name="local",
    )(projected, taps, product, table)


def long_finish(q, y, state, high, low, segs):
    groups, own, channels = q.shape
    seg = own // segs
    whole = pl.BlockSpec((1, own, LANES), lambda i, x: (x, 0, i))
    decay = pl.BlockSpec((seg, PER * ORDER), lambda i, x: (0, i))
    return pl.pallas_call(
        functools.partial(finish_kernel, segs),
        grid=(channels // LANES, groups),
        in_specs=[
            whole,
            whole,
            pl.BlockSpec((1, segs, ORDER, LANES), lambda i, x: (x, 0, 0, i)),
            decay,
            decay,
        ],
        out_specs=whole,
        out_shape=jax.ShapeDtypeStruct((groups, own, channels), bf16),
        compiler_params=params(),
        cost_estimate=cost(2**28, 8 * 2**20),
        name="finish",
    )(q, y, state, high, low)


def split_high_low(value):
    high = lax.reduce_precision(value, 8, 7)
    return high.astype(bf16), (value - high).astype(bf16)


def shift_seq(value, steps):
    count = lax.axis_size("seq")
    return lax.ppermute(value, "seq", [(s, s + steps) for s in range(count - steps)])


def pair_stack(mine, other, index):
    first = index == 0
    return jnp.stack([jnp.where(first, mine, other), jnp.where(first, other, mine)])


def turn(value, steps, cores):
    count = lax.axis_size("seq")
    return lax.ppermute(
        value, "seq", [((s + steps * cores) % count, s) for s in range(count)]
    )


def spread_pieces(piece, chips, cores):
    return [piece] + [turn(piece, step, cores) for step in range(1, chips)]


def body(
    stream_in,
    mr_features,
    mr_short,
    medium_taps,
    mr_out_weight,
    li_gain,
    li_in_weight,
    li_short,
    li_rates,
    li_residues,
):
    rows = stream_in.shape[0]
    width = stream_in.shape[1]
    channels = mr_features.shape[2]
    tensors = lax.axis_size("tensor")
    cores = 2 if tensors == 1 and lax.axis_size("seq") % 4 == 0 else 1
    wide = 2 if cores == 2 and lax.axis_size("parts") == 2 else 1
    share = cores * wide
    count = lax.axis_size("seq")
    chips = count // cores
    seq_rank = lax.axis_index("seq")
    core = seq_rank % cores
    side = lax.axis_index("parts") if wide == 2 else 0
    tensor_rank = lax.axis_index("tensor")
    swap_pairs = [(s, s ^ 1) for s in range(count)]

    def swap_core(value):
        return lax.ppermute(value, "seq", swap_pairs)

    def swap_side(value):
        return lax.ppermute(value, "parts", [(0, 1), (1, 0)])

    part = channels // share
    quarter = side * cores + core
    filters = part // GROUP
    first_filter = tensor_rank * (channels // GROUP) + quarter * filters

    features = jnp.transpose(mr_features, (1, 0, 2))
    rim = jnp.concatenate(
        [features[1, rows - BLK - RIM :], features[2, rows - BLK - RIM :], features[0, rows - RIM :]]
    )
    rim = shift_seq(rim, 1)

    if cores == 2:
        out_pieces = spread_pieces(mr_out_weight, chips, cores)
        weight = li_in_weight.reshape(-1, 3, share, part)
        mine = lax.dynamic_index_in_dim(weight, side * cores + core, 2, keepdims=False)
        theirs = lax.dynamic_index_in_dim(weight, side * cores + 1 - core, 2, keepdims=False)
        mine = mine.reshape(-1, 3 * part)
        other = swap_core(theirs.reshape(-1, 3 * part))
        in_piece = pair_stack(mine, other, core).reshape(-1, 3 * part)
    else:
        out_weight = lax.all_gather(mr_out_weight, "seq", axis=1, tiled=True)
        in_weight = lax.all_gather(li_in_weight, "seq", axis=0, tiled=True).reshape(width, -1)

    local_taps = lax.dynamic_slice_in_dim(
        medium_taps, tensor_rank * (channels // GROUP), channels // GROUP, 1
    )
    medium_table = toeplitz(jnp.pad(local_taps.T, ((0, 0), (0, 2 * BLK - MEDIUM))))
    rates = lax.dynamic_slice_in_dim(li_rates, first_filter, filters, 0)
    residues = lax.dynamic_slice_in_dim(li_residues, first_filter, filters, 0)
    scaled = residues * jnp.sqrt(2.0 * rates / ORDER)
    steps = jnp.arange(rows, dtype=f32)
    spread = scaled.reshape(1, -1) * jnp.exp(-rates.reshape(1, -1) * steps[:, None])
    long_table = toeplitz(jnp.sum(spread.reshape(rows, filters, ORDER), axis=-1).T)
    spread_high, spread_low = split_high_low(spread)
    tail = jnp.exp(-rates.reshape(-1, 1) * (rows - steps)[None, :])
    tail_high, tail_low = split_high_low(tail)
    by_channel = jnp.repeat(rates.T, GROUP, axis=1)
    seg_decay = jnp.exp(-by_channel * rows)
    gaps = jnp.arange(1, chips)
    gap_decays = jnp.where(
        (seq_rank // cores >= gaps)[:, None, None],
        jnp.exp(-by_channel * (rows * cores * (gaps - 1)).astype(f32)[:, None, None]),
        0.0,
    )
    short_part = lax.dynamic_slice_in_dim(li_short, quarter * part, part, 2)
    short_part = jnp.transpose(short_part, (1, 0, 2))

    if cores == 2:
        in_piece, medium_table = lax.optimization_barrier((in_piece, medium_table))
        in_pieces = spread_pieces(in_piece, chips, cores)
    gated = medium(features, rim, jnp.transpose(mr_short, (1, 0, 2)), medium_table)

    if cores == 2:
        where = jnp.stack([seq_rank // cores, core, jnp.asarray(side, jnp.int32)])
        mine, theirs = out_projection(gated, swap_core(gated), out_pieces)
        stream, normed = stream_norm(where, mine, swap_core(theirs), stream_in, li_gain[None])
        sources = []
        for own in [normed] + ([swap_side(normed)] if wide == 2 else []):
            sources += [own, swap_core(own)]
        ahead = jnp.stack(
            [
                jnp.where(core == 1, sources[i][:, rows - RIM :], sources[i + 1][:, rows - RIM :])
                for i in range(0, len(sources), 2)
            ]
        )
        ahead = jnp.roll(turn(ahead, -1, cores), -1, axis=1)
        projected = in_projection(where, ahead, sources, in_pieces)
    else:
        summed = lax.psum(jnp.dot(gated, out_weight, preferred_element_type=f32), "tensor")
        stream = (stream_in.astype(f32) + summed).astype(bf16)
        widened = stream.astype(f32)
        mean_square = jnp.mean(widened * widened, axis=-1, keepdims=True)
        normed = (widened * lax.rsqrt(mean_square + 1e-06) * li_gain).astype(bf16)
        ahead = shift_seq(normed[rows - RIM :], 1)
        projected = jnp.dot(
            jnp.concatenate([ahead, normed]), in_weight, preferred_element_type=f32
        ).astype(bf16)[None]

    product, added = long_product(projected, short_part, tail_high, tail_low, cores)
    state = added[:, 0]
    for seg in range(1, cores):
        state = state * seg_decay + added[:, seg]
    start = 0.0
    for gap in range(1, chips):
        start = start + gap_decays[gap - 1] * turn(state, -gap, cores)
    starts = [start]
    for seg in range(1, cores):
        starts.append(starts[-1] * seg_decay + added[:, seg - 1])
    q, y = long_local(projected, short_part, product, long_table, cores)
    gated_li = long_finish(q, y, jnp.stack(starts, axis=1), spread_high, spread_low, cores)

    result = gated_li
    if wide == 2:
        mine = lax.dynamic_index_in_dim(result, side, 0, keepdims=False)
        theirs = lax.dynamic_index_in_dim(result, 1 - side, 0, keepdims=False)
        result = pair_stack(mine, swap_side(theirs), side)
    if cores == 2:
        result = result.reshape(wide, cores, rows, part)
        mine = lax.dynamic_index_in_dim(result, core, 1, keepdims=False)
        theirs = lax.dynamic_index_in_dim(result, 1 - core, 1, keepdims=False)
        result = pair_stack(mine, swap_core(theirs), core)
        result = jnp.transpose(result, (2, 1, 0, 3)).reshape(rows, channels)
    else:
        result = result.reshape(rows, channels)
    return (stream, result)


def solution(mesh):
    placed = (
        P(("parts", "seq"), None),
        P(("parts", "seq"), None, "tensor"),
        P(None, None, "tensor"),
        P(),
        P("tensor", "seq"),
        P(),
        P("seq", None, "tensor"),
        P(None, None, "tensor"),
        P(),
        P(),
    )
    return jax.shard_map(
        body,
        mesh=mesh,
        in_specs=placed,
        out_specs=(P(("parts", "seq"), None), P(("parts", "seq"), "tensor")),
        check_vma=False,
    )
```

```python
import functools

import jax
import jax.numpy as jnp
from jax import lax
from jax.experimental import pallas as pl
from jax.experimental.pallas import tpu as pltpu
from jax.sharding import PartitionSpec as P

GROUP = 16
ORDER = 16
SHORT = 7
MEDIUM = 128
BLK = 128
LANES = 128
PER = LANES // GROUP
RIM = 16
bf16 = jnp.bfloat16
f32 = jnp.float32


def cost(flops, nbytes):
    return pl.CostEstimate(flops=flops, bytes_accessed=nbytes, transcendentals=0)


def params():
    return pltpu.CompilerParams(vmem_limit_bytes=40 * 1024 * 1024)


def toeplitz_kernel(base_ref, out_ref):
    row = lax.broadcasted_iota(jnp.int32, (BLK, 2 * BLK), 0)
    col = lax.broadcasted_iota(jnp.int32, (BLK, 2 * BLK), 1)
    causal = col <= row + BLK
    for g in range(PER):
        wide = jnp.broadcast_to(base_ref[g : g + 1, :], (BLK, 2 * BLK))
        rolled = pltpu.roll(wide, 0, 1, stride=1, stride_axis=0)
        out_ref[g * BLK : (g + 1) * BLK, :] = jnp.where(causal, rolled, 0.0).astype(bf16)


def toeplitz(kernel_taps):
    filters = kernel_taps.shape[0]
    base = jnp.roll(kernel_taps[:, ::-1], BLK + 1, axis=1)
    return pl.pallas_call(
        toeplitz_kernel,
        grid=(filters // PER,),
        in_specs=[pl.BlockSpec((PER, 2 * BLK), lambda i: (i, 0))],
        out_specs=pl.BlockSpec((PER * BLK, 2 * BLK), lambda i: (i, 0)),
        out_shape=jax.ShapeDtypeStruct((filters * BLK, 2 * BLK), bf16),
        compiler_params=params(),
        cost_estimate=cost(0, filters * BLK * 2 * BLK * 4),
        name="toeplitz",
    )(base)


def pick(result):
    lane = lax.broadcasted_iota(jnp.int32, (BLK, 2 * LANES), 1) % LANES // GROUP
    total = result[:BLK]
    for g in range(1, PER):
        total = jnp.where(lane == g, result[g * BLK : (g + 1) * BLK], total)
    return total


def two_blocks(table, before, first, second):
    wide = jnp.concatenate(
        [jnp.concatenate([before, first], axis=0), jnp.concatenate([first, second], axis=0)], axis=1
    )
    result = pick(jnp.dot(table, wide, preferred_element_type=f32))
    return result[:, :LANES], result[:, LANES:]


def fir(values, taps, start, length):
    total = taps[0:1] * values[start : start + length]
    for lagged in range(1, SHORT):
        total = total + taps[lagged : lagged + 1] * values[start - lagged : start - lagged + length]
    return total


def medium_kernel(cores, x_ref, rim_ref, taps_ref, table_ref, *refs):
    if cores == 2:
        wo_ref, wi_ref, out_ref, wo_all, wi_all, send_sem, recv_sem = refs
        count = lax.axis_size("seq")
        me = lax.axis_index("seq")
        chips = count // cores

        def copies():
            made = []
            for which, (own, everyone) in enumerate(((wo_ref, wo_all), (wi_ref, wi_all))):
                for step in range(1, chips):
                    made.append(
                        pltpu.make_async_remote_copy(
                            src_ref=own,
                            dst_ref=everyone.at[step - 1],
                            send_sem=send_sem.at[which, step - 1],
                            recv_sem=recv_sem.at[which, step - 1],
                            device_id={"seq": lax.rem(me + count - step * cores, count)},
                            device_id_type=pl.DeviceIdType.MESH,
                        )
                    )
            return made

        @pl.when(pl.program_id(0) == 0)
        def _():
            barrier = pltpu.get_barrier_semaphore()
            for step in range(1, chips):
                pl.semaphore_signal(
                    barrier,
                    inc=1,
                    device_id={"seq": lax.rem(me + step * cores, count)},
                    device_id_type=pl.DeviceIdType.MESH,
                )
            pl.semaphore_wait(barrier, chips - 1)
            for copy in copies():
                copy.start()
    else:
        (out_ref,) = refs
    own = x_ref.shape[1]
    ahead = BLK + RIM

    def joined(at, length, i):
        return jnp.concatenate([rim_ref[at : at + length], x_ref[i]], axis=0).astype(f32)

    q = fir(joined(2 * ahead, RIM, 0), taps_ref[0], RIM, own)
    k = fir(joined(0, ahead, 1), taps_ref[1], RIM, own + BLK)
    v = fir(joined(ahead, ahead, 2), taps_ref[2], RIM, own + BLK)
    product = (k * v).astype(bf16)
    table = table_ref[...]
    for n in range(0, own // BLK, 2):
        part = [product[(n + j) * BLK : (n + j + 1) * BLK] for j in range(3)]
        y0, y1 = two_blocks(table, *part)
        out_ref[n * BLK : (n + 1) * BLK] = (q[n * BLK : (n + 1) * BLK] * y0).astype(bf16)
        out_ref[(n + 1) * BLK : (n + 2) * BLK] = (q[(n + 1) * BLK : (n + 2) * BLK] * y1).astype(bf16)


    if cores == 2:

        @pl.when(pl.program_id(0) == pl.num_programs(0) - 1)
        def _():
            for copy in copies():
                copy.wait()


def medium(features, rim, taps, table, weights, cores):
    _, own, channels = features.shape
    chips = lax.axis_size("seq") // cores
    others = [jax.ShapeDtypeStruct((chips - 1,) + w.shape, w.dtype) for w in weights]
    anywhere = pl.BlockSpec(memory_space=pl.ANY)
    scratch = [pltpu.SemaphoreType.DMA((2, chips - 1))] * 2 if weights else []
    extra = dict(collective_id=0, has_side_effects=True) if weights else {}
    return pl.pallas_call(
        functools.partial(medium_kernel, cores),
        grid=(channels // LANES,),
        in_specs=[
            pl.BlockSpec((3, own, LANES), lambda i: (0, 0, i)),
            pl.BlockSpec((rim.shape[0], LANES), lambda i: (0, i)),
            pl.BlockSpec((3, SHORT, LANES), lambda i: (0, 0, i)),
            pl.BlockSpec((PER * BLK, 2 * BLK), lambda i: (i, 0)),
        ]
        + [anywhere] * len(weights),
        out_specs=[pl.BlockSpec((own, LANES), lambda i: (0, i))] + [anywhere] * len(weights),
        out_shape=[jax.ShapeDtypeStruct((own, channels), bf16)] + others,
        scratch_shapes=scratch,
        compiler_params=pltpu.CompilerParams(vmem_limit_bytes=40 * 1024 * 1024, **extra),
        cost_estimate=cost(channels // LANES * 2 * 1024 * 256 * 256, 16 * 2**20),
        name="medium",
    )(features, rim, taps, table, *weights)


def out_kernel(a_ref, b_ref, own_ref, all_ref, mine, theirs):
    pieces = [own_ref] + [all_ref.at[j] for j in range(all_ref.shape[0])]
    for n in range(0, len(pieces), 2):
        weight = jnp.concatenate([pieces[n][...], pieces[n + 1][...]], axis=1)
        for source, target in ((a_ref, mine), (b_ref, theirs)):
            result = jnp.dot(source[...], weight, preferred_element_type=f32)
            half = result.shape[1] // 2
            target[n] = result[:, :half]
            target[n + 1] = result[:, half:]


def out_projection(gated, other, own, everyone):
    rows = gated.shape[0]
    shape = jax.ShapeDtypeStruct((everyone.shape[0] + 1, rows, own.shape[1]), f32)
    return pl.pallas_call(
        out_kernel,
        out_shape=[shape, shape],
        compiler_params=params(),
        cost_estimate=cost(2**31, 9 * 2**20),
        name="out_projection",
    )(gated, other, own, everyone)


def stream_kernel(where_ref, mine_ref, recv_ref, in_ref, gain_ref, stream_ref, normed_ref):
    chips, rows, piece = mine_ref.shape
    chip, core = where_ref[0], where_ref[1]
    total = jnp.zeros((rows, 1), f32)
    kept = []
    for j in range(chips):
        columns = pl.ds(pl.multiple_of((chip + j) % chips * 2 * piece, 2 * piece), 2 * piece)
        mine, recv = mine_ref[j], recv_ref[j]
        first = jnp.where(core == 0, mine, recv)
        second = jnp.where(core == 0, recv, mine)
        update = jnp.concatenate([first, second], axis=1)
        value = (in_ref[:, columns].astype(f32) + update).astype(bf16)
        stream_ref[:, columns] = value
        value = value.astype(f32)
        total = total + jnp.sum(value * value, axis=1, keepdims=True)
        kept.append((columns, value))
    scale = lax.rsqrt(total / (chips * 2 * piece) + 1e-06)
    for j in range(chips):
        columns, value = kept[j]
        normed_ref[j] = (value * scale * gain_ref[:, columns]).astype(bf16)


def stream_norm(where, mine, recv, stream_in, gain):
    chips, rows, piece = mine.shape
    width = stream_in.shape[1]
    step = 64
    pieces = pl.BlockSpec((chips, step, piece), lambda i: (0, i, 0))
    whole = pl.BlockSpec((step, width), lambda i: (i, 0))
    return pl.pallas_call(
        stream_kernel,
        grid=(rows // step,),
        in_specs=[
            pl.BlockSpec(memory_space=pltpu.SMEM),
            pieces,
            pieces,
            whole,
            pl.BlockSpec((1, width), lambda i: (0, 0)),
        ],
        out_specs=[whole, pl.BlockSpec((chips, step, 2 * piece), lambda i: (0, i, 0))],
        out_shape=[
            jax.ShapeDtypeStruct((rows, width), bf16),
            jax.ShapeDtypeStruct((chips, rows, 2 * piece), bf16),
        ],
        compiler_params=params(),
        cost_estimate=cost(2**22, 6 * 2**20),
        name="stream_norm",
    )(where, mine, recv, stream_in, gain)


def in_kernel(wide, chips, where_ref, ahead_ref, *refs):
    sources, (own_ref, all_ref, out_ref) = refs[: 2 * wide], refs[2 * wide :]
    pieces = [own_ref] + [all_ref.at[j] for j in range(chips - 1)]
    side, core, chip = where_ref[2], where_ref[1], where_ref[0]
    rows = sources[0].shape[1]

    def times(value):
        total = jnp.dot(value(0), pieces[0][...], preferred_element_type=f32)
        for j in range(1, chips):
            total = total + jnp.dot(value(j), pieces[j][...], preferred_element_type=f32)
        return total

    for off_side in range(wide):
        at = (side + off_side) % wide
        front = times(lambda j: ahead_ref[off_side, j])
        out_ref[at, :RIM] = jnp.where(chip > 0, front, 0.0).astype(bf16)
        for off_core in range(2):
            start = pl.multiple_of(RIM + (core + off_core) % 2 * rows, RIM)
            result = times(lambda j: sources[off_side * 2 + off_core][j])
            out_ref[at, pl.ds(start, rows)] = result.astype(bf16)


def in_projection(where, ahead, sources, own, everyone):
    wide = len(sources) // 2
    chips, rows, depth = sources[0].shape
    columns = own.shape[1]
    step = 256
    fixed = pl.BlockSpec((chips, rows, depth), lambda n: (0, 0, 0))
    total = RIM + 2 * rows
    return pl.pallas_call(
        functools.partial(in_kernel, wide, chips),
        grid=(columns // step,),
        in_specs=[
            pl.BlockSpec(memory_space=pltpu.SMEM),
            pl.BlockSpec(ahead.shape, lambda n: (0, 0, 0, 0)),
        ]
        + [fixed] * len(sources)
        + [
            pl.BlockSpec((depth, step), lambda n: (0, n)),
            pl.BlockSpec((chips - 1, depth, step), lambda n: (0, 0, n)),
        ],
        out_specs=pl.BlockSpec((wide, total, step), lambda n: (0, 0, n)),
        out_shape=jax.ShapeDtypeStruct((wide, total, columns), bf16),
        compiler_params=params(),
        cost_estimate=cost(2 * wide * total * chips * depth * columns, 14 * 2**20),
        name="in_projection",
    )(where, ahead, *sources, own, everyone)


def product_kernel(segs, k_ref, v_ref, taps_ref, high_ref, low_ref, product_ref, state_ref):
    rows = k_ref.shape[1] - RIM
    seg = rows // segs
    k = fir(k_ref[0].astype(f32), taps_ref[1], RIM, rows)
    v = fir(v_ref[0].astype(f32), taps_ref[2], RIM, rows)
    product = (k * v).astype(bf16)
    product_ref[0] = product
    lane = lax.broadcasted_iota(jnp.int32, (ORDER, LANES), 1) // GROUP
    for s in range(segs):
        part = product[s * seg : (s + 1) * seg]
        sums = jnp.dot(high_ref[...], part, preferred_element_type=f32) + jnp.dot(
            low_ref[...], part, preferred_element_type=f32
        )
        total = sums[:ORDER]
        for g in range(1, PER):
            total = jnp.where(lane == g, sums[g * ORDER : (g + 1) * ORDER], total)
        state_ref[0, s] = total


def local_kernel(segs, q_ref, taps_ref, product_ref, table_ref, q_out, y_out):
    rows = q_ref.shape[1] - RIM
    seg = rows // segs
    q_out[0] = fir(q_ref[0].astype(f32), taps_ref[0], RIM, rows)
    zeros = jnp.zeros((BLK, LANES), bf16)
    table = table_ref[...]
    for s in range(segs):
        first = product_ref[0, s * seg : s * seg + BLK]
        second = product_ref[0, s * seg + BLK : (s + 1) * seg]
        y0, y1 = two_blocks(table, zeros, first, second)
        y_out[0, s * seg : s * seg + BLK] = y0
        y_out[0, s * seg + BLK : (s + 1) * seg] = y1


def finish_kernel(segs, q_ref, y_ref, state_ref, high_ref, low_ref, out_ref):
    seg = q_ref.shape[1] // segs
    row = lax.broadcasted_iota(jnp.int32, (LANES, LANES), 0) // ORDER
    lane = lax.broadcasted_iota(jnp.int32, (LANES, LANES), 1) // GROUP
    for s in range(segs):
        state = jnp.concatenate([state_ref[0, s]] * PER, axis=0)
        state = jnp.where(row == lane, state, 0.0)
        state_high = state.astype(bf16)
        state_low = (state - state_high.astype(f32)).astype(bf16)
        at = slice(s * seg, (s + 1) * seg)
        y = y_ref[0, at]
        y = y + jnp.dot(high_ref[...], state_high, preferred_element_type=f32)
        y = y + jnp.dot(high_ref[...], state_low, preferred_element_type=f32)
        y = y + jnp.dot(low_ref[...], state_high, preferred_element_type=f32)
        out_ref[0, at] = (q_ref[0, at] * y.astype(bf16).astype(f32)).astype(bf16)


def long_product(projected, taps, high, low, segs):
    groups, rows, channels = projected.shape
    channels //= 3
    blocks = channels // LANES
    own = rows - RIM
    seg = own // segs
    return pl.pallas_call(
        functools.partial(product_kernel, segs),
        grid=(blocks, groups),
        in_specs=[
            pl.BlockSpec((1, rows, LANES), lambda i, x: (x, 0, blocks + i)),
            pl.BlockSpec((1, rows, LANES), lambda i, x: (x, 0, 2 * blocks + i)),
            pl.BlockSpec((3, SHORT, LANES), lambda i, x: (0, 0, i)),
            pl.BlockSpec((PER * ORDER, seg), lambda i, x: (i, 0)),
            pl.BlockSpec((PER * ORDER, seg), lambda i, x: (i, 0)),
        ],
        out_specs=[
            pl.BlockSpec((1, own, LANES), lambda i, x: (x, 0, i)),
            pl.BlockSpec((1, segs, ORDER, LANES), lambda i, x: (x, 0, 0, i)),
        ],
        out_shape=[
            jax.ShapeDtypeStruct((groups, own, channels), bf16),
            jax.ShapeDtypeStruct((groups, segs, ORDER, channels), f32),
        ],
        compiler_params=params(),
        cost_estimate=cost(2**28, 8 * 2**20),
        name="product",
    )(projected, projected, taps, high, low)


def long_local(projected, taps, product, table, segs):
    groups, rows, channels = projected.shape
    channels //= 3
    own = rows - RIM
    whole = pl.BlockSpec((1, own, LANES), lambda i, x: (x, 0, i))
    return pl.pallas_call(
        functools.partial(local_kernel, segs),
        grid=(channels // LANES, groups),
        in_specs=[
            pl.BlockSpec((1, rows, LANES), lambda i, x: (x, 0, i)),
            pl.BlockSpec((3, SHORT, LANES), lambda i, x: (0, 0, i)),
            whole,
            pl.BlockSpec((PER * BLK, 2 * BLK), lambda i, x: (i, 0)),
        ],
        out_specs=[whole, whole],
        out_shape=[jax.ShapeDtypeStruct((groups, own, channels), f32)] * 2,
        compiler_params=params(),
        cost_estimate=cost(2**31, 16 * 2**20),
        name="local",
    )(projected, taps, product, table)


def long_finish(q, y, state, high, low, segs):
    groups, own, channels = q.shape
    seg = own // segs
    whole = pl.BlockSpec((1, own, LANES), lambda i, x: (x, 0, i))
    decay = pl.BlockSpec((seg, PER * ORDER), lambda i, x: (0, i))
    return pl.pallas_call(
        functools.partial(finish_kernel, segs),
        grid=(channels // LANES, groups),
        in_specs=[
            whole,
            whole,
            pl.BlockSpec((1, segs, ORDER, LANES), lambda i, x: (x, 0, 0, i)),
            decay,
            decay,
        ],
        out_specs=whole,
        out_shape=jax.ShapeDtypeStruct((groups, own, channels), bf16),
        compiler_params=params(),
        cost_estimate=cost(2**28, 8 * 2**20),
        name="finish",
    )(q, y, state, high, low)


def split_high_low(value):
    high = lax.reduce_precision(value, 8, 7)
    return high.astype(bf16), (value - high).astype(bf16)


def shift_seq(value, steps):
    count = lax.axis_size("seq")
    return lax.ppermute(value, "seq", [(s, s + steps) for s in range(count - steps)])


def pair_stack(mine, other, index):
    first = index == 0
    return jnp.stack([jnp.where(first, mine, other), jnp.where(first, other, mine)])


def turn(value, steps, cores):
    count = lax.axis_size("seq")
    return lax.ppermute(
        value, "seq", [((s + steps * cores) % count, s) for s in range(count)]
    )


def body(
    stream_in,
    mr_features,
    mr_short,
    medium_taps,
    mr_out_weight,
    li_gain,
    li_in_weight,
    li_short,
    li_rates,
    li_residues,
):
    rows = stream_in.shape[0]
    width = stream_in.shape[1]
    channels = mr_features.shape[2]
    tensors = lax.axis_size("tensor")
    cores = 2 if tensors == 1 and lax.axis_size("seq") % 4 == 0 else 1
    wide = 2 if cores == 2 and lax.axis_size("parts") == 2 else 1
    share = cores * wide
    count = lax.axis_size("seq")
    chips = count // cores
    seq_rank = lax.axis_index("seq")
    core = seq_rank % cores
    side = lax.axis_index("parts") if wide == 2 else 0
    tensor_rank = lax.axis_index("tensor")
    swap_pairs = [(s, s ^ 1) for s in range(count)]

    def swap_core(value):
        return lax.ppermute(value, "seq", swap_pairs)

    def swap_side(value):
        return lax.ppermute(value, "parts", [(0, 1), (1, 0)])

    part = channels // share
    quarter = side * cores + core
    filters = part // GROUP
    first_filter = tensor_rank * (channels // GROUP) + quarter * filters

    features = jnp.transpose(mr_features, (1, 0, 2))
    rim = jnp.concatenate(
        [features[1, rows - BLK - RIM :], features[2, rows - BLK - RIM :], features[0, rows - RIM :]]
    )
    rim = shift_seq(rim, 1)

    if cores == 2:
        weight = li_in_weight.reshape(-1, 3, share, part)
        mine = lax.dynamic_index_in_dim(weight, side * cores + core, 2, keepdims=False)
        theirs = lax.dynamic_index_in_dim(weight, side * cores + 1 - core, 2, keepdims=False)
        mine = mine.reshape(-1, 3 * part)
        other = swap_core(theirs.reshape(-1, 3 * part))
        in_piece = pair_stack(mine, other, core).reshape(-1, 3 * part)
    else:
        out_weight = lax.all_gather(mr_out_weight, "seq", axis=1, tiled=True)
        in_weight = lax.all_gather(li_in_weight, "seq", axis=0, tiled=True).reshape(width, -1)

    local_taps = lax.dynamic_slice_in_dim(
        medium_taps, tensor_rank * (channels // GROUP), channels // GROUP, 1
    )
    medium_table = toeplitz(jnp.pad(local_taps.T, ((0, 0), (0, 2 * BLK - MEDIUM))))
    rates = lax.dynamic_slice_in_dim(li_rates, first_filter, filters, 0)
    residues = lax.dynamic_slice_in_dim(li_residues, first_filter, filters, 0)
    scaled = residues * jnp.sqrt(2.0 * rates / ORDER)
    steps = jnp.arange(rows, dtype=f32)
    spread = scaled.reshape(1, -1) * jnp.exp(-rates.reshape(1, -1) * steps[:, None])
    long_table = toeplitz(jnp.sum(spread.reshape(rows, filters, ORDER), axis=-1).T)
    spread_high, spread_low = split_high_low(spread)
    tail = jnp.exp(-rates.reshape(-1, 1) * (rows - steps)[None, :])
    tail_high, tail_low = split_high_low(tail)
    by_channel = jnp.repeat(rates.T, GROUP, axis=1)
    seg_decay = jnp.exp(-by_channel * rows)
    gaps = jnp.arange(1, chips)
    gap_decays = jnp.where(
        (seq_rank // cores >= gaps)[:, None, None],
        jnp.exp(-by_channel * (rows * cores * (gaps - 1)).astype(f32)[:, None, None]),
        0.0,
    )
    short_part = lax.dynamic_slice_in_dim(li_short, quarter * part, part, 2)
    short_part = jnp.transpose(short_part, (1, 0, 2))

    gated, *gathered = medium(
        features,
        rim,
        jnp.transpose(mr_short, (1, 0, 2)),
        medium_table,
        [mr_out_weight, in_piece] if cores == 2 else [],
        cores,
    )

    if cores == 2:
        where = jnp.stack([seq_rank // cores, core, jnp.asarray(side, jnp.int32)])
        mine, theirs = out_projection(gated, swap_core(gated), mr_out_weight, gathered[0])
        stream, normed = stream_norm(where, mine, swap_core(theirs), stream_in, li_gain[None])
        sources = []
        for own in [normed] + ([swap_side(normed)] if wide == 2 else []):
            sources += [own, swap_core(own)]
        ahead = jnp.stack(
            [
                jnp.where(core == 1, sources[i][:, rows - RIM :], sources[i + 1][:, rows - RIM :])
                for i in range(0, len(sources), 2)
            ]
        )
        ahead = jnp.roll(turn(ahead, -1, cores), -1, axis=1)
        tables = (long_table, spread_high, spread_low, tail_high, tail_low, seg_decay, gap_decays)
        ahead, short_part, tables = lax.optimization_barrier((ahead, short_part, tables))
        long_table, spread_high, spread_low, tail_high, tail_low, seg_decay, gap_decays = tables
        projected = in_projection(where, ahead, sources, in_piece, gathered[1])
    else:
        summed = lax.psum(jnp.dot(gated, out_weight, preferred_element_type=f32), "tensor")
        stream = (stream_in.astype(f32) + summed).astype(bf16)
        widened = stream.astype(f32)
        mean_square = jnp.mean(widened * widened, axis=-1, keepdims=True)
        normed = (widened * lax.rsqrt(mean_square + 1e-06) * li_gain).astype(bf16)
        ahead = shift_seq(normed[rows - RIM :], 1)
        projected = jnp.dot(
            jnp.concatenate([ahead, normed]), in_weight, preferred_element_type=f32
        ).astype(bf16)[None]

    product, added = long_product(projected, short_part, tail_high, tail_low, cores)
    state = added[:, 0]
    for seg in range(1, cores):
        state = state * seg_decay + added[:, seg]
    start = 0.0
    for gap in range(1, chips):
        start = start + gap_decays[gap - 1] * turn(state, -gap, cores)
    starts = [start]
    for seg in range(1, cores):
        starts.append(starts[-1] * seg_decay + added[:, seg - 1])
    q, y = long_local(projected, short_part, product, long_table, cores)
    gated_li = long_finish(q, y, jnp.stack(starts, axis=1), spread_high, spread_low, cores)

    result = gated_li
    if wide == 2:
        mine = lax.dynamic_index_in_dim(result, side, 0, keepdims=False)
        theirs = lax.dynamic_index_in_dim(result, 1 - side, 0, keepdims=False)
        result = pair_stack(mine, swap_side(theirs), side)
    if cores == 2:
        result = result.reshape(wide, cores, rows, part)
        mine = lax.dynamic_index_in_dim(result, core, 1, keepdims=False)
        theirs = lax.dynamic_index_in_dim(result, 1 - core, 1, keepdims=False)
        result = pair_stack(mine, swap_core(theirs), core)
        result = jnp.transpose(result, (2, 1, 0, 3)).reshape(rows, channels)
    else:
        result = result.reshape(rows, channels)
    return (stream, result)


def solution(mesh):
    placed = (
        P(("parts", "seq"), None),
        P(("parts", "seq"), None, "tensor"),
        P(None, None, "tensor"),
        P(),
        P("tensor", "seq"),
        P(),
        P("seq", None, "tensor"),
        P(None, None, "tensor"),
        P(),
        P(),
    )
    return jax.shard_map(
        body,
        mesh=mesh,
        in_specs=placed,
        out_specs=(P(("parts", "seq"), None), P(("parts", "seq"), "tensor")),
        check_vma=False,
    )
```

```python
import functools

import jax
import jax.numpy as jnp
from jax import lax
from jax.experimental import pallas as pl
from jax.experimental.pallas import tpu as pltpu
from jax.sharding import PartitionSpec as P

GROUP = 16
ORDER = 16
SHORT = 7
MEDIUM = 128
BLK = 128
LANES = 128
PER = LANES // GROUP
RIM = 16
bf16 = jnp.bfloat16
f32 = jnp.float32


def cost(flops, nbytes):
    return pl.CostEstimate(flops=flops, bytes_accessed=nbytes, transcendentals=0)


def params():
    return pltpu.CompilerParams(vmem_limit_bytes=40 * 1024 * 1024)


def toeplitz_kernel(base_ref, out_ref):
    row = lax.broadcasted_iota(jnp.int32, (BLK, 2 * BLK), 0)
    col = lax.broadcasted_iota(jnp.int32, (BLK, 2 * BLK), 1)
    causal = col <= row + BLK
    for g in range(PER):
        wide = jnp.broadcast_to(base_ref[g : g + 1, :], (BLK, 2 * BLK))
        rolled = pltpu.roll(wide, 0, 1, stride=1, stride_axis=0)
        out_ref[g * BLK : (g + 1) * BLK, :] = jnp.where(causal, rolled, 0.0).astype(bf16)


def toeplitz(kernel_taps):
    filters = kernel_taps.shape[0]
    base = jnp.roll(kernel_taps[:, ::-1], BLK + 1, axis=1)
    return pl.pallas_call(
        toeplitz_kernel,
        grid=(filters // PER,),
        in_specs=[pl.BlockSpec((PER, 2 * BLK), lambda i: (i, 0))],
        out_specs=pl.BlockSpec((PER * BLK, 2 * BLK), lambda i: (i, 0)),
        out_shape=jax.ShapeDtypeStruct((filters * BLK, 2 * BLK), bf16),
        compiler_params=params(),
        cost_estimate=cost(0, filters * BLK * 2 * BLK * 4),
        name="toeplitz",
    )(base)


def pick(result):
    lane = lax.broadcasted_iota(jnp.int32, (BLK, 2 * LANES), 1) % LANES // GROUP
    total = result[:BLK]
    for g in range(1, PER):
        total = jnp.where(lane == g, result[g * BLK : (g + 1) * BLK], total)
    return total


def two_blocks(table, before, first, second):
    wide = jnp.concatenate(
        [jnp.concatenate([before, first], axis=0), jnp.concatenate([first, second], axis=0)], axis=1
    )
    result = pick(jnp.dot(table, wide, preferred_element_type=f32))
    return result[:, :LANES], result[:, LANES:]


def fir(values, taps, start, length):
    total = taps[0:1] * values[start : start + length]
    for lagged in range(1, SHORT):
        total = total + taps[lagged : lagged + 1] * values[start - lagged : start - lagged + length]
    return total


def medium_kernel(cores, x_ref, rim_ref, taps_ref, table_ref, *refs):
    if cores == 2:
        wo_ref, wi_ref, out_ref, wo_all, wi_all, send_sem, recv_sem = refs
        count = lax.axis_size("seq")
        me = lax.axis_index("seq")
        chips = count // cores

        chip, core = me // cores, lax.rem(me, cores)
        place = chip // 2 + lax.rem(chip, 2) * (chips - 1 - 2 * (chip // 2))

        def chip_at(spot):
            spot = lax.rem(spot + 2 * chips, chips)
            column = spot // (chips // 2)
            return 2 * (spot + column * (chips - 1 - 2 * spot)) + column

        def copies(step):
            made = []
            for way, sign in enumerate((1, -1)):
                owner, target = chip_at(place - sign * step), chip_at(place + sign)
                for which, (own, everyone) in enumerate(((wo_ref, wo_all), (wi_ref, wi_all))):
                    half = own.shape[0] // 2
                    rows = pl.ds(way * half, half)
                    here = lax.rem(owner - chip + chips, chips) - 1
                    there = lax.rem(owner - target + chips, chips) - 1
                    made.append(
                        pltpu.make_async_remote_copy(
                            src_ref=everyone.at[here, rows] if step else own.at[rows],
                            dst_ref=everyone.at[there, rows],
                            send_sem=send_sem.at[2 * way + which, step],
                            recv_sem=recv_sem.at[2 * way + which, step],
                            device_id={"seq": target * cores + core},
                            device_id_type=pl.DeviceIdType.MESH,
                        )
                    )
            return made

        @pl.when(pl.program_id(0) == 0)
        def _():
            barrier = pltpu.get_barrier_semaphore()
            for sign in (1, -1):
                pl.semaphore_signal(
                    barrier,
                    inc=1,
                    device_id={"seq": chip_at(place + sign) * cores + core},
                    device_id_type=pl.DeviceIdType.MESH,
                )
            pl.semaphore_wait(barrier, 2)
            for copy in copies(0):
                copy.start()
    else:
        (out_ref,) = refs
    own = x_ref.shape[1]
    ahead = BLK + RIM

    def joined(at, length, i):
        return jnp.concatenate([rim_ref[at : at + length], x_ref[i]], axis=0).astype(f32)

    q = fir(joined(2 * ahead, RIM, 0), taps_ref[0], RIM, own)
    k = fir(joined(0, ahead, 1), taps_ref[1], RIM, own + BLK)
    v = fir(joined(ahead, ahead, 2), taps_ref[2], RIM, own + BLK)
    product = (k * v).astype(bf16)
    table = table_ref[...]
    for n in range(0, own // BLK, 2):
        part = [product[(n + j) * BLK : (n + j + 1) * BLK] for j in range(3)]
        y0, y1 = two_blocks(table, *part)
        out_ref[n * BLK : (n + 1) * BLK] = (q[n * BLK : (n + 1) * BLK] * y0).astype(bf16)
        out_ref[(n + 1) * BLK : (n + 2) * BLK] = (q[(n + 1) * BLK : (n + 2) * BLK] * y1).astype(bf16)


    if cores == 2:

        @pl.when(pl.program_id(0) == pl.num_programs(0) - 1)
        def _():
            for step in range(1, chips - 1):
                for before, copy in zip(copies(step - 1), copies(step)):
                    before.wait_recv()
                    copy.start()
            for copy in copies(chips - 2):
                copy.wait_recv()
            for step in range(chips - 1):
                for copy in copies(step):
                    copy.wait_send()


def medium(features, rim, taps, table, weights, cores):
    _, own, channels = features.shape
    chips = lax.axis_size("seq") // cores
    others = [jax.ShapeDtypeStruct((chips - 1,) + w.shape, w.dtype) for w in weights]
    anywhere = pl.BlockSpec(memory_space=pl.ANY)
    scratch = [pltpu.SemaphoreType.DMA((4, chips - 1))] * 2 if weights else []
    extra = dict(collective_id=0, has_side_effects=True) if weights else {}
    return pl.pallas_call(
        functools.partial(medium_kernel, cores),
        grid=(channels // LANES,),
        in_specs=[
            pl.BlockSpec((3, own, LANES), lambda i: (0, 0, i)),
            pl.BlockSpec((rim.shape[0], LANES), lambda i: (0, i)),
            pl.BlockSpec((3, SHORT, LANES), lambda i: (0, 0, i)),
            pl.BlockSpec((PER * BLK, 2 * BLK), lambda i: (i, 0)),
        ]
        + [anywhere] * len(weights),
        out_specs=[pl.BlockSpec((own, LANES), lambda i: (0, i))] + [anywhere] * len(weights),
        out_shape=[jax.ShapeDtypeStruct((own, channels), bf16)] + others,
        scratch_shapes=scratch,
        compiler_params=pltpu.CompilerParams(vmem_limit_bytes=40 * 1024 * 1024, **extra),
        cost_estimate=cost(channels // LANES * 2 * 1024 * 256 * 256, 16 * 2**20),
        name="medium",
    )(features, rim, taps, table, *weights)


def out_kernel(a_ref, b_ref, own_ref, all_ref, mine, theirs):
    pieces = [own_ref] + [all_ref.at[j] for j in range(all_ref.shape[0])]
    for n in range(0, len(pieces), 2):
        weight = jnp.concatenate([pieces[n][...], pieces[n + 1][...]], axis=1)
        for source, target in ((a_ref, mine), (b_ref, theirs)):
            result = jnp.dot(source[...], weight, preferred_element_type=f32)
            half = result.shape[1] // 2
            target[n] = result[:, :half]
            target[n + 1] = result[:, half:]


def out_projection(gated, other, own, everyone):
    rows = gated.shape[0]
    shape = jax.ShapeDtypeStruct((everyone.shape[0] + 1, rows, own.shape[1]), f32)
    return pl.pallas_call(
        out_kernel,
        out_shape=[shape, shape],
        compiler_params=params(),
        cost_estimate=cost(2**31, 9 * 2**20),
        name="out_projection",
    )(gated, other, own, everyone)


def stream_kernel(where_ref, mine_ref, recv_ref, in_ref, gain_ref, stream_ref, normed_ref):
    chips, rows, piece = mine_ref.shape
    chip, core = where_ref[0], where_ref[1]
    total = jnp.zeros((rows, 1), f32)
    kept = []
    for j in range(chips):
        columns = pl.ds(pl.multiple_of((chip + j) % chips * 2 * piece, 2 * piece), 2 * piece)
        mine, recv = mine_ref[j], recv_ref[j]
        first = jnp.where(core == 0, mine, recv)
        second = jnp.where(core == 0, recv, mine)
        update = jnp.concatenate([first, second], axis=1)
        value = (in_ref[:, columns].astype(f32) + update).astype(bf16)
        stream_ref[:, columns] = value
        value = value.astype(f32)
        total = total + jnp.sum(value * value, axis=1, keepdims=True)
        kept.append((columns, value))
    scale = lax.rsqrt(total / (chips * 2 * piece) + 1e-06)
    for j in range(chips):
        columns, value = kept[j]
        normed_ref[j] = (value * scale * gain_ref[:, columns]).astype(bf16)


def stream_norm(where, mine, recv, stream_in, gain):
    chips, rows, piece = mine.shape
    width = stream_in.shape[1]
    step = 64
    pieces = pl.BlockSpec((chips, step, piece), lambda i: (0, i, 0))
    whole = pl.BlockSpec((step, width), lambda i: (i, 0))
    return pl.pallas_call(
        stream_kernel,
        grid=(rows // step,),
        in_specs=[
            pl.BlockSpec(memory_space=pltpu.SMEM),
            pieces,
            pieces,
            whole,
            pl.BlockSpec((1, width), lambda i: (0, 0)),
        ],
        out_specs=[whole, pl.BlockSpec((chips, step, 2 * piece), lambda i: (0, i, 0))],
        out_shape=[
            jax.ShapeDtypeStruct((rows, width), bf16),
            jax.ShapeDtypeStruct((chips, rows, 2 * piece), bf16),
        ],
        compiler_params=params(),
        cost_estimate=cost(2**22, 6 * 2**20),
        name="stream_norm",
    )(where, mine, recv, stream_in, gain)


def in_kernel(wide, chips, where_ref, ahead_ref, *refs):
    sources, (own_ref, all_ref, out_ref) = refs[: 2 * wide], refs[2 * wide :]
    pieces = [own_ref] + [all_ref.at[j] for j in range(chips - 1)]
    side, core, chip = where_ref[2], where_ref[1], where_ref[0]
    rows = sources[0].shape[1]

    def times(value):
        total = jnp.dot(value(0), pieces[0][...], preferred_element_type=f32)
        for j in range(1, chips):
            total = total + jnp.dot(value(j), pieces[j][...], preferred_element_type=f32)
        return total

    for off_side in range(wide):
        at = (side + off_side) % wide
        front = times(lambda j: ahead_ref[off_side, j])
        out_ref[at, :RIM] = jnp.where(chip > 0, front, 0.0).astype(bf16)
        for off_core in range(2):
            start = pl.multiple_of(RIM + (core + off_core) % 2 * rows, RIM)
            result = times(lambda j: sources[off_side * 2 + off_core][j])
            out_ref[at, pl.ds(start, rows)] = result.astype(bf16)


def in_projection(where, ahead, sources, own, everyone):
    wide = len(sources) // 2
    chips, rows, depth = sources[0].shape
    columns = own.shape[1]
    step = 256
    fixed = pl.BlockSpec((chips, rows, depth), lambda n: (0, 0, 0))
    total = RIM + 2 * rows
    return pl.pallas_call(
        functools.partial(in_kernel, wide, chips),
        grid=(columns // step,),
        in_specs=[
            pl.BlockSpec(memory_space=pltpu.SMEM),
            pl.BlockSpec(ahead.shape, lambda n: (0, 0, 0, 0)),
        ]
        + [fixed] * len(sources)
        + [
            pl.BlockSpec((depth, step), lambda n: (0, n)),
            pl.BlockSpec((chips - 1, depth, step), lambda n: (0, 0, n)),
        ],
        out_specs=pl.BlockSpec((wide, total, step), lambda n: (0, 0, n)),
        out_shape=jax.ShapeDtypeStruct((wide, total, columns), bf16),
        compiler_params=params(),
        cost_estimate=cost(2 * wide * total * chips * depth * columns, 14 * 2**20),
        name="in_projection",
    )(where, ahead, *sources, own, everyone)


def product_kernel(segs, k_ref, v_ref, taps_ref, high_ref, low_ref, product_ref, state_ref):
    rows = k_ref.shape[1] - RIM
    seg = rows // segs
    k = fir(k_ref[0].astype(f32), taps_ref[1], RIM, rows)
    v = fir(v_ref[0].astype(f32), taps_ref[2], RIM, rows)
    product = (k * v).astype(bf16)
    product_ref[0] = product
    lane = lax.broadcasted_iota(jnp.int32, (ORDER, LANES), 1) // GROUP
    for s in range(segs):
        part = product[s * seg : (s + 1) * seg]
        sums = jnp.dot(high_ref[...], part, preferred_element_type=f32) + jnp.dot(
            low_ref[...], part, preferred_element_type=f32
        )
        total = sums[:ORDER]
        for g in range(1, PER):
            total = jnp.where(lane == g, sums[g * ORDER : (g + 1) * ORDER], total)
        state_ref[0, s] = total


def local_kernel(segs, q_ref, taps_ref, product_ref, table_ref, q_out, y_out):
    rows = q_ref.shape[1] - RIM
    seg = rows // segs
    q_out[0] = fir(q_ref[0].astype(f32), taps_ref[0], RIM, rows)
    zeros = jnp.zeros((BLK, LANES), bf16)
    table = table_ref[...]
    for s in range(segs):
        first = product_ref[0, s * seg : s * seg + BLK]
        second = product_ref[0, s * seg + BLK : (s + 1) * seg]
        y0, y1 = two_blocks(table, zeros, first, second)
        y_out[0, s * seg : s * seg + BLK] = y0
        y_out[0, s * seg + BLK : (s + 1) * seg] = y1


def finish_kernel(segs, q_ref, y_ref, state_ref, high_ref, low_ref, out_ref):
    seg = q_ref.shape[1] // segs
    row = lax.broadcasted_iota(jnp.int32, (LANES, LANES), 0) // ORDER
    lane = lax.broadcasted_iota(jnp.int32, (LANES, LANES), 1) // GROUP
    for s in range(segs):
        state = jnp.concatenate([state_ref[0, s]] * PER, axis=0)
        state = jnp.where(row == lane, state, 0.0)
        state_high = state.astype(bf16)
        state_low = (state - state_high.astype(f32)).astype(bf16)
        at = slice(s * seg, (s + 1) * seg)
        y = y_ref[0, at]
        y = y + jnp.dot(high_ref[...], state_high, preferred_element_type=f32)
        y = y + jnp.dot(high_ref[...], state_low, preferred_element_type=f32)
        y = y + jnp.dot(low_ref[...], state_high, preferred_element_type=f32)
        out_ref[0, at] = (q_ref[0, at] * y.astype(bf16).astype(f32)).astype(bf16)


def long_product(projected, taps, high, low, segs):
    groups, rows, channels = projected.shape
    channels //= 3
    blocks = channels // LANES
    own = rows - RIM
    seg = own // segs
    return pl.pallas_call(
        functools.partial(product_kernel, segs),
        grid=(blocks, groups),
        in_specs=[
            pl.BlockSpec((1, rows, LANES), lambda i, x: (x, 0, blocks + i)),
            pl.BlockSpec((1, rows, LANES), lambda i, x: (x, 0, 2 * blocks + i)),
            pl.BlockSpec((3, SHORT, LANES), lambda i, x: (0, 0, i)),
            pl.BlockSpec((PER * ORDER, seg), lambda i, x: (i, 0)),
            pl.BlockSpec((PER * ORDER, seg), lambda i, x: (i, 0)),
        ],
        out_specs=[
            pl.BlockSpec((1, own, LANES), lambda i, x: (x, 0, i)),
            pl.BlockSpec((1, segs, ORDER, LANES), lambda i, x: (x, 0, 0, i)),
        ],
        out_shape=[
            jax.ShapeDtypeStruct((groups, own, channels), bf16),
            jax.ShapeDtypeStruct((groups, segs, ORDER, channels), f32),
        ],
        compiler_params=params(),
        cost_estimate=cost(2**28, 8 * 2**20),
        name="product",
    )(projected, projected, taps, high, low)


def long_local(projected, taps, product, table, segs):
    groups, rows, channels = projected.shape
    channels //= 3
    own = rows - RIM
    whole = pl.BlockSpec((1, own, LANES), lambda i, x: (x, 0, i))
    return pl.pallas_call(
        functools.partial(local_kernel, segs),
        grid=(channels // LANES, groups),
        in_specs=[
            pl.BlockSpec((1, rows, LANES), lambda i, x: (x, 0, i)),
            pl.BlockSpec((3, SHORT, LANES), lambda i, x: (0, 0, i)),
            whole,
            pl.BlockSpec((PER * BLK, 2 * BLK), lambda i, x: (i, 0)),
        ],
        out_specs=[whole, whole],
        out_shape=[jax.ShapeDtypeStruct((groups, own, channels), f32)] * 2,
        compiler_params=params(),
        cost_estimate=cost(2**31, 16 * 2**20),
        name="local",
    )(projected, taps, product, table)


def long_finish(q, y, state, high, low, segs):
    groups, own, channels = q.shape
    seg = own // segs
    whole = pl.BlockSpec((1, own, LANES), lambda i, x: (x, 0, i))
    decay = pl.BlockSpec((seg, PER * ORDER), lambda i, x: (0, i))
    return pl.pallas_call(
        functools.partial(finish_kernel, segs),
        grid=(channels // LANES, groups),
        in_specs=[
            whole,
            whole,
            pl.BlockSpec((1, segs, ORDER, LANES), lambda i, x: (x, 0, 0, i)),
            decay,
            decay,
        ],
        out_specs=whole,
        out_shape=jax.ShapeDtypeStruct((groups, own, channels), bf16),
        compiler_params=params(),
        cost_estimate=cost(2**28, 8 * 2**20),
        name="finish",
    )(q, y, state, high, low)


def split_high_low(value):
    high = lax.reduce_precision(value, 8, 7)
    return high.astype(bf16), (value - high).astype(bf16)


def shift_seq(value, steps):
    count = lax.axis_size("seq")
    return lax.ppermute(value, "seq", [(s, s + steps) for s in range(count - steps)])


def pair_stack(mine, other, index):
    first = index == 0
    return jnp.stack([jnp.where(first, mine, other), jnp.where(first, other, mine)])


def turn(value, steps, cores):
    count = lax.axis_size("seq")
    return lax.ppermute(
        value, "seq", [((s + steps * cores) % count, s) for s in range(count)]
    )


def body(
    stream_in,
    mr_features,
    mr_short,
    medium_taps,
    mr_out_weight,
    li_gain,
    li_in_weight,
    li_short,
    li_rates,
    li_residues,
):
    rows = stream_in.shape[0]
    width = stream_in.shape[1]
    channels = mr_features.shape[2]
    tensors = lax.axis_size("tensor")
    cores = 2 if tensors == 1 and lax.axis_size("seq") % 4 == 0 else 1
    wide = 2 if cores == 2 and lax.axis_size("parts") == 2 else 1
    share = cores * wide
    count = lax.axis_size("seq")
    chips = count // cores
    seq_rank = lax.axis_index("seq")
    core = seq_rank % cores
    side = lax.axis_index("parts") if wide == 2 else 0
    tensor_rank = lax.axis_index("tensor")
    swap_pairs = [(s, s ^ 1) for s in range(count)]

    def swap_core(value):
        return lax.ppermute(value, "seq", swap_pairs)

    def swap_side(value):
        return lax.ppermute(value, "parts", [(0, 1), (1, 0)])

    part = channels // share
    quarter = side * cores + core
    filters = part // GROUP
    first_filter = tensor_rank * (channels // GROUP) + quarter * filters

    features = jnp.transpose(mr_features, (1, 0, 2))
    rim = jnp.concatenate(
        [features[1, rows - BLK - RIM :], features[2, rows - BLK - RIM :], features[0, rows - RIM :]]
    )
    rim = shift_seq(rim, 1)

    if cores == 2:
        weight = li_in_weight.reshape(-1, 3, share, part)
        mine = lax.dynamic_index_in_dim(weight, side * cores + core, 2, keepdims=False)
        theirs = lax.dynamic_index_in_dim(weight, side * cores + 1 - core, 2, keepdims=False)
        mine = mine.reshape(-1, 3 * part)
        other = swap_core(theirs.reshape(-1, 3 * part))
        in_piece = pair_stack(mine, other, core).reshape(-1, 3 * part)
    else:
        out_weight = lax.all_gather(mr_out_weight, "seq", axis=1, tiled=True)
        in_weight = lax.all_gather(li_in_weight, "seq", axis=0, tiled=True).reshape(width, -1)

    local_taps = lax.dynamic_slice_in_dim(
        medium_taps, tensor_rank * (channels // GROUP), channels // GROUP, 1
    )
    medium_table = toeplitz(jnp.pad(local_taps.T, ((0, 0), (0, 2 * BLK - MEDIUM))))
    rates = lax.dynamic_slice_in_dim(li_rates, first_filter, filters, 0)
    residues = lax.dynamic_slice_in_dim(li_residues, first_filter, filters, 0)
    scaled = residues * jnp.sqrt(2.0 * rates / ORDER)
    steps = jnp.arange(rows, dtype=f32)
    spread = scaled.reshape(1, -1) * jnp.exp(-rates.reshape(1, -1) * steps[:, None])
    long_table = toeplitz(jnp.sum(spread.reshape(rows, filters, ORDER), axis=-1).T)
    spread_high, spread_low = split_high_low(spread)
    tail = jnp.exp(-rates.reshape(-1, 1) * (rows - steps)[None, :])
    tail_high, tail_low = split_high_low(tail)
    by_channel = jnp.repeat(rates.T, GROUP, axis=1)
    seg_decay = jnp.exp(-by_channel * rows)
    gaps = jnp.arange(1, chips)
    gap_decays = jnp.where(
        (seq_rank // cores >= gaps)[:, None, None],
        jnp.exp(-by_channel * (rows * cores * (gaps - 1)).astype(f32)[:, None, None]),
        0.0,
    )
    short_part = lax.dynamic_slice_in_dim(li_short, quarter * part, part, 2)
    short_part = jnp.transpose(short_part, (1, 0, 2))

    gated, *gathered = medium(
        features,
        rim,
        jnp.transpose(mr_short, (1, 0, 2)),
        medium_table,
        [mr_out_weight, in_piece] if cores == 2 else [],
        cores,
    )

    if cores == 2:
        where = jnp.stack([seq_rank // cores, core, jnp.asarray(side, jnp.int32)])
        mine, theirs = out_projection(gated, swap_core(gated), mr_out_weight, gathered[0])
        stream, normed = stream_norm(where, mine, swap_core(theirs), stream_in, li_gain[None])
        sources = []
        for own in [normed] + ([swap_side(normed)] if wide == 2 else []):
            sources += [own, swap_core(own)]
        ahead = jnp.stack(
            [
                jnp.where(core == 1, sources[i][:, rows - RIM :], sources[i + 1][:, rows - RIM :])
                for i in range(0, len(sources), 2)
            ]
        )
        ahead = jnp.roll(turn(ahead, -1, cores), -1, axis=1)
        tables = (long_table, spread_high, spread_low, tail_high, tail_low, seg_decay, gap_decays)
        ahead, short_part, tables = lax.optimization_barrier((ahead, short_part, tables))
        long_table, spread_high, spread_low, tail_high, tail_low, seg_decay, gap_decays = tables
        projected = in_projection(where, ahead, sources, in_piece, gathered[1])
    else:
        summed = lax.psum(jnp.dot(gated, out_weight, preferred_element_type=f32), "tensor")
        stream = (stream_in.astype(f32) + summed).astype(bf16)
        widened = stream.astype(f32)
        mean_square = jnp.mean(widened * widened, axis=-1, keepdims=True)
        normed = (widened * lax.rsqrt(mean_square + 1e-06) * li_gain).astype(bf16)
        ahead = shift_seq(normed[rows - RIM :], 1)
        projected = jnp.dot(
            jnp.concatenate([ahead, normed]), in_weight, preferred_element_type=f32
        ).astype(bf16)[None]

    product, added = long_product(projected, short_part, tail_high, tail_low, cores)
    state = added[:, 0]
    for seg in range(1, cores):
        state = state * seg_decay + added[:, seg]
    start = 0.0
    for gap in range(1, chips):
        start = start + gap_decays[gap - 1] * turn(state, -gap, cores)
    starts = [start]
    for seg in range(1, cores):
        starts.append(starts[-1] * seg_decay + added[:, seg - 1])
    q, y = long_local(projected, short_part, product, long_table, cores)
    gated_li = long_finish(q, y, jnp.stack(starts, axis=1), spread_high, spread_low, cores)

    result = gated_li
    if wide == 2:
        mine = lax.dynamic_index_in_dim(result, side, 0, keepdims=False)
        theirs = lax.dynamic_index_in_dim(result, 1 - side, 0, keepdims=False)
        result = pair_stack(mine, swap_side(theirs), side)
    if cores == 2:
        result = result.reshape(wide, cores, rows, part)
        mine = lax.dynamic_index_in_dim(result, core, 1, keepdims=False)
        theirs = lax.dynamic_index_in_dim(result, 1 - core, 1, keepdims=False)
        result = pair_stack(mine, swap_core(theirs), core)
        result = jnp.transpose(result, (2, 1, 0, 3)).reshape(rows, channels)
    else:
        result = result.reshape(rows, channels)
    return (stream, result)


def solution(mesh):
    placed = (
        P(("parts", "seq"), None),
        P(("parts", "seq"), None, "tensor"),
        P(None, None, "tensor"),
        P(),
        P("tensor", "seq"),
        P(),
        P("seq", None, "tensor"),
        P(None, None, "tensor"),
        P(),
        P(),
    )
    return jax.shard_map(
        body,
        mesh=mesh,
        in_specs=placed,
        out_specs=(P(("parts", "seq"), None), P(("parts", "seq"), "tensor")),
        check_vma=False,
    )
```
